32 devices in a mesh: seq: 8 (over y, x, core), head: 4 (over z).
Axes of the slice: x: 2, y: 2, z: 4, core: 2. Of those that a mesh axis runs over, the one named last changes fastest.
Arguments:
- lin_query: bfloat16 [1024, 2048], P('seq', 'head'), may hold values from -0.52734375 to 0.52734375
- lin_key: bfloat16 [1024, 2048], P('seq', 'head'), may hold values from -0.52734375 to 0.52734375
- lin_value: bfloat16 [1024, 2048], P('seq', 'head'), may hold values from -6 to 6
- log_decay: float32 [16, 1024], P('head', 'seq'), may hold values from -1.5 to 0
- out_gate: bfloat16 [1024, 2048], P('seq', 'head'), may hold values from -8 to 8
- norm_gain: float32 [2048], P('head'), may hold values from 0.25 to 1.75
- soft_query: bfloat16 [1024, 2048], P('seq', 'head'), may hold values from -8 to 8
- soft_key: bfloat16 [1024, 256], P('seq'), may hold values from -6 to 6
- soft_value: bfloat16 [1024, 256], P('seq'), may hold values from -6 to 6
- segment_of: int32 [8], replicated, may hold values from 0 to 7, each once
Outputs:
- lin_out: bfloat16 [1024, 2048], P('seq', 'head')
- soft_out: bfloat16 [1024, 2048], P('seq', 'head')
The draws below stay inside these ranges and needn't reach their ends.
Inputs may be any that keep to these rules, and one draw needn't show every extreme that they name: `segment_of`: each segment number stands once.
All inputs are finite; a program needn't handle non-finite values.
Results may differ from the reference program's by a relative error of at most 0.008.
Values may be sent and summed in bfloat16 or wider, within the bound.
A program may use at most 128 MiB of HBM per device.

```python
import math
import jax
import jax.numpy as jnp
from jax import lax

HEAD_DIM = 128
Q_PER_KV = 8
TOK_DEV = 128
QUERY_HEAD_COUNT = 16
KV_HEADS = 2
TOKEN_COUNT = 1024
SEGMENTS = 8


def draw_log_decay(key, part):
    random_key_root, random_key_noise, random_key_block, random_key_spike, random_key_depth = jax.random.split(key, 5)
    log_low = math.log(0.2 / TOKEN_COUNT)
    log_high = math.log(1.0 / 30.0)
    base_rate = jnp.exp(jax.random.uniform(random_key_root, (QUERY_HEAD_COUNT, 1), jnp.float32, log_low, log_high))
    jitter = jax.random.uniform(random_key_noise, (QUERY_HEAD_COUNT, TOKEN_COUNT), jnp.float32, 0.5, 2.0)
    block_count = TOKEN_COUNT // TOK_DEV
    block_log = jax.random.uniform(random_key_block, (QUERY_HEAD_COUNT, block_count, 1), jnp.float32, math.log(0.5), math.log(2.0))
    block_factor = jnp.broadcast_to(jnp.exp(block_log), (QUERY_HEAD_COUNT, block_count, TOK_DEV)).reshape(QUERY_HEAD_COUNT, TOKEN_COUNT)
    spike_strike = jax.random.uniform(random_key_spike, (QUERY_HEAD_COUNT, TOKEN_COUNT), jnp.float32, 0.0, 1.0) < 3.0 / TOKEN_COUNT
    spike_depth = jax.random.uniform(random_key_depth, (QUERY_HEAD_COUNT, TOKEN_COUNT), jnp.float32, 0.2, 0.7)
    steady_level = -(base_rate * jitter * block_factor)
    return steady_level + jnp.where(spike_strike, jnp.log(1.0 - spike_depth), 0.0)


def draw_soft_query(key, part):
    width = QUERY_HEAD_COUNT * HEAD_DIM
    drawn_key = jax.random.fold_in(key, 11)
    return jnp.clip(jax.random.normal(drawn_key, (TOKEN_COUNT, width), jnp.float32), -6.0, 6.0).astype(jnp.bfloat16)


def draw_soft_key(key, part):
    width = KV_HEADS * HEAD_DIM
    drawn_key = jax.random.fold_in(key, 12)
    return jnp.clip(jax.random.normal(drawn_key, (TOKEN_COUNT, width), jnp.float32), -6.0, 6.0).astype(jnp.bfloat16)


def block_scale(rng, extent, cuts, low, high):
    factor_of = 1.0
    for axis_at, shards_of in cuts:
        steps = jax.random.uniform(jax.random.fold_in(jax.random.fold_in(rng, 6), axis_at), (shards_of,), jnp.float32, low / len(cuts), high / len(cuts))
        factor_of = factor_of * jnp.repeat(jnp.exp(steps), extent[axis_at] // shards_of).reshape((-1,) + (1,) * (len(extent) - 1 - axis_at))
    return factor_of


def scatter_about(key, extent, scale, reach, pieces=(), kind=jnp.bfloat16):
    values = jax.random.normal(key, extent, jnp.float32) * scale
    if len(pieces) > 0:
        values = block_scale(key, extent, pieces, -0.22, 0.18) * values
    return jnp.clip(values, min=-reach, max=reach).astype(kind)


def setup_inputs(seed: int = 0) -> dict:
    splits = jax.random.split(jax.random.key(seed), 11)
    return {
        "lin_query": scatter_about(splits[0], (TOKEN_COUNT, QUERY_HEAD_COUNT * HEAD_DIM), (HEAD_DIM ** -0.5), 0.52734375, ((0, 8), (1, 4))),
        "lin_key": scatter_about(splits[1], (TOKEN_COUNT, QUERY_HEAD_COUNT * HEAD_DIM), (HEAD_DIM ** -0.5), 0.52734375, ((0, 8), (1, 4))),
        "lin_value": scatter_about(splits[2], (TOKEN_COUNT, QUERY_HEAD_COUNT * HEAD_DIM), 1.0, 6.0, ((0, 8), (1, 4))),
        "log_decay": draw_log_decay(jax.random.fold_in(splits[10], 71), 0),
        "out_gate": scatter_about(splits[4], (TOKEN_COUNT, QUERY_HEAD_COUNT * HEAD_DIM), 1.5, 8.0, ((0, 8), (1, 4))),
        "norm_gain": jnp.clip(1.0 + 0.15 * jax.random.normal(splits[5], (QUERY_HEAD_COUNT * HEAD_DIM,), jnp.float32), 0.25, 1.75),
        "soft_query": draw_soft_query(jax.random.fold_in(splits[10], 71), 0),
        "soft_key": draw_soft_key(jax.random.fold_in(splits[10], 71), 0),
        "soft_value": scatter_about(splits[8], (TOKEN_COUNT, KV_HEADS * HEAD_DIM), 1.0, 6.0, ((0, 8),)),
        "segment_of": jax.random.permutation(splits[9], SEGMENTS).astype(jnp.int32),
    }


norm_eps = 1e-06

def rounded(values_in):
    return lax.optimization_barrier(values_in.astype(jnp.bfloat16)).astype(jnp.float32)

def decay_weights(cumulative):
    row_count = cumulative.shape[1]
    positions = jnp.arange(row_count, dtype=jnp.int32)
    causal_mask = positions[:, None] >= positions[None, :]
    spread = cumulative[:, :, None] - cumulative[:, None, :]
    return jnp.where(causal_mask[None], jnp.exp(jnp.where(causal_mask[None], spread, 0.0)), 0.0)

def lightning_layer(lin_query, lin_key, lin_value, log_decay, out_gate, norm_gain):
    blocks = TOKEN_COUNT // TOK_DEV

    def to_blocks(array):
        return array.reshape(blocks, TOK_DEV, QUERY_HEAD_COUNT, HEAD_DIM).astype(jnp.float32)
    decays = log_decay.reshape(QUERY_HEAD_COUNT, blocks, TOK_DEV).transpose(1, 0, 2)

    def advance(memory, inputs):
        query_heads, key_heads, value_heads, block_log = inputs
        cumulative = jnp.cumsum(block_log, axis=1)
        scores = jnp.einsum('thd,shd->hts', query_heads, key_heads)
        mixing = rounded(scores * decay_weights(cumulative))
        inside = jnp.einsum('hts,shd->thd', mixing, value_heads)
        tail_decay = jnp.exp(cumulative[:, -1:] - cumulative)
        weighted_keys = key_heads * tail_decay.T[:, :, None]
        local_memory = jnp.einsum('thd,the->hde', weighted_keys, value_heads, precision=lax.Precision.HIGHEST)
        lifted = query_heads * jnp.exp(cumulative).T[:, :, None]
        earlier_part = jnp.einsum('thd,hde->the', lifted, memory, precision=lax.Precision.HIGHEST)
        new_memory = jnp.exp(cumulative[:, -1])[:, None, None] * memory + local_memory
        return (new_memory, inside + earlier_part)
    start_memory = jnp.zeros((QUERY_HEAD_COUNT, HEAD_DIM, HEAD_DIM), jnp.float32)
    final_memory, mixed_out = lax.scan(advance, start_memory, (to_blocks(lin_query), to_blocks(lin_key), to_blocks(lin_value), decays))
    mixed_out = mixed_out.reshape(TOKEN_COUNT, QUERY_HEAD_COUNT * HEAD_DIM)
    inverse_rms = lax.rsqrt(lax.optimization_barrier(jnp.mean(mixed_out * mixed_out, axis=1)) + norm_eps)
    gated = mixed_out * inverse_rms[:, None] * norm_gain[None, :] * jax.nn.sigmoid(out_gate.astype(jnp.float32))
    return gated.astype(jnp.bfloat16)

def softmax_layer(soft_query, soft_key, soft_value, segment_of):
    row_ids = jnp.arange(TOKEN_COUNT, dtype=jnp.int32)
    positions = segment_of[row_ids // TOK_DEV] * TOK_DEV + row_ids % TOK_DEV
    query_heads = soft_query.reshape(TOKEN_COUNT, KV_HEADS, Q_PER_KV, HEAD_DIM).transpose(1, 0, 2, 3)
    key_heads = soft_key.reshape(TOKEN_COUNT, KV_HEADS, HEAD_DIM).transpose(1, 0, 2)
    value_heads = soft_value.reshape(TOKEN_COUNT, KV_HEADS, HEAD_DIM).transpose(1, 0, 2)
    blocks = TOKEN_COUNT // TOK_DEV
    score_scale = HEAD_DIM ** (-0.5)

    def one_head(inputs):
        head_query, head_key, head_value = inputs
        key_float = head_key.astype(jnp.float32)
        value_float = head_value.astype(jnp.float32)

        def one_block(block_index):
            block_query = lax.dynamic_slice_in_dim(head_query, block_index * TOK_DEV, TOK_DEV, 0)
            block_pos = lax.dynamic_slice_in_dim(positions, block_index * TOK_DEV, TOK_DEV, 0)
            logits = jnp.einsum('tgd,sd->gts', block_query.astype(jnp.float32), key_float) * score_scale
            visible = positions[None, :] <= block_pos[:, None]
            logits = jnp.where(visible[None], logits, -1e+30)
            row_peak = lax.optimization_barrier(jnp.max(logits, axis=2))
            weights_now = jnp.where(visible[None], jnp.exp(logits - row_peak[:, :, None]), 0.0)
            totals = lax.optimization_barrier(jnp.sum(weights_now, axis=2))
            summed = jnp.einsum('gts,sd->gtd', rounded(weights_now), value_float)
            return (summed / totals[:, :, None]).transpose(1, 0, 2)
        return lax.map(one_block, jnp.arange(blocks, dtype=jnp.int32))
    outputs = lax.map(one_head, (query_heads, key_heads, value_heads))
    return outputs.transpose(1, 2, 0, 3, 4).reshape(TOKEN_COUNT, QUERY_HEAD_COUNT * HEAD_DIM).astype(jnp.bfloat16)

def reference(lin_query, lin_key, lin_value, log_decay, out_gate, norm_gain, soft_query, soft_key, soft_value, segment_of):
    lin_out = lightning_layer(lin_query, lin_key, lin_value, log_decay, out_gate, norm_gain)
    soft_out = softmax_layer(soft_query, soft_key, soft_value, segment_of)
    return (lin_out, soft_out)
```

```python
import functools

import jax
import jax.numpy as jnp
from jax import lax
from jax.experimental import pallas as pl
from jax.experimental.pallas import tpu as pltpu
from jax.sharding import PartitionSpec as P

HEAD_DIM = 128
Q_PER_KV = 8
NORM_EPS = 1e-06
MESH = pl.DeviceIdType.MESH
F32 = jnp.float32
BF16 = jnp.bfloat16
NT = (((1,), (1,)), ((), ()))
TN = (((0,), (0,)), ((), ()))
HIGH = lax.Precision.HIGHEST


def dot(a, b, dims=(((1,), (0,)), ((), ())), precision=None):
    return lax.dot_general(a, b, dims, preferred_element_type=F32, precision=precision)


def each(count, body):
    if count <= 8:
        for i in range(count):
            body(i)
    else:
        lax.fori_loop(0, count, lambda i, _: (body(i), 0)[1], 0)


def kernel(
    n,
    nh,
    lq_hbm,
    lk_hbm,
    lv_hbm,
    ld_hbm,
    gate_hbm,
    gain_ref,
    sq_hbm,
    sk_hbm,
    sv_hbm,
    seg_ref,
    lin_ref,
    soft_ref,
    lq,
    lk,
    lv,
    gate,
    sq,
    qs,
    kv,
    logs,
    mem_own,
    mem_sib,
    tot_own,
    tot_all,
    pre,
    ent_own,
    ent_sib,
    mixed,
    sums,
    top,
    acc,
    den,
    in_sem,
    kv_send,
    kv_recv,
    fwd_send,
    log_send,
    log_recv,
    mem_send,
    mem_recv,
    tot_send,
    tot_recv,
    ent_send,
    ent_recv,
    sum_send,
    sum_recv,
):
    chips = n // 2
    me = lax.axis_index("seq")
    col = lax.axis_index("head")
    chip, core = me // 2, me % 2
    sib = chip * 2 + 1 - core
    tokens = lq.shape[0]
    heads = lq.shape[1] // HEAD_DIM
    half = heads // 2
    share = pl.multiple_of((col * heads // Q_PER_KV) * HEAD_DIM, HEAD_DIM)

    barrier = pltpu.get_barrier_semaphore()

    def greet(i):
        pl.semaphore_signal(
            barrier, inc=1, device_id=((me + 1 + i) % n, col), device_id_type=MESH
        )

    def greet_col(i):
        pl.semaphore_signal(
            barrier, inc=1, device_id=(me, (col + 1 + i) % nh), device_id_type=MESH
        )

    each(n - 1, greet)
    each(nh - 1, greet_col)

    def local(src, dst, at):
        copy = pltpu.make_async_copy(src, dst, in_sem.at[at])
        copy.start()
        return copy

    get_ld = local(ld_hbm, logs.at[me], 0)
    get_lk = local(lk_hbm, lk, 1)
    get_lv = local(lv_hbm, lv, 2)
    get_lq = local(lq_hbm, lq, 3)
    get_sk = local(sk_hbm.at[:, pl.ds(share, HEAD_DIM)], kv.at[me, 0], 4)
    get_sv = local(sv_hbm.at[:, pl.ds(share, HEAD_DIM)], kv.at[me, 1], 5)
    get_sq = local(sq_hbm, sq, 6)
    get_gate = local(gate_hbm, gate, 7)

    def remote(src, dst, send, recv, seq_to, col_to):
        return pltpu.make_async_remote_copy(
            src_ref=src,
            dst_ref=dst,
            send_sem=send,
            recv_sem=recv,
            device_id=(seq_to, col_to),
            device_id_type=MESH,
        )

    get_ld.wait()
    get_sk.wait()
    get_sv.wait()
    pl.semaphore_wait(barrier, n - 1 + nh - 1)

    def log_copy(i):
        return remote(
            logs.at[me],
            logs.at[me],
            log_send.at[i],
            log_recv.at[i],
            (me + 1 + i) % n,
            col,
        )

    def kv_copy(i, part, to):
        return remote(
            kv.at[me, part],
            kv.at[me, part],
            kv_send.at[i, part],
            kv_recv.at[i, part],
            to,
            col,
        )

    def far(i):
        return ((chip + 1 + i) % chips) * 2 + core

    def near(i):
        return (chip + chips - 1 - i) % chips

    each(n - 1, lambda i: log_copy(i).start())

    def kv_go(i):
        kv_copy(i, 0, far(i)).start()
        kv_copy(i, 1, far(i)).start()

    each(chips - 1, kv_go)
    kv_copy(chips - 1, 0, sib).start()
    kv_copy(chips - 1, 1, sib).start()

    rows = lax.broadcasted_iota(jnp.int32, (tokens, tokens), 0)
    cols = lax.broadcasted_iota(jnp.int32, (tokens, tokens), 1)
    causal = rows >= cols
    lower = jnp.where(causal, 1.0, 0.0).astype(F32)
    decay = logs[me]
    cum_row = dot(decay, lower, NT, HIGH)
    cum_col = dot(lower, decay, NT, HIGH)
    tail = jnp.exp(cum_col[tokens - 1 : tokens, :] - cum_col)
    lift = jnp.exp(cum_col)

    def cut(h):
        return slice(h * HEAD_DIM, (h + 1) * HEAD_DIM)

    get_lk.wait()
    get_lv.wait()
    for h in range(heads):
        weighted = (lk[:, cut(h)].astype(F32) * tail[:, h : h + 1]).astype(BF16)
        mem_own[h] = dot(weighted, lv[:, cut(h)], TN).astype(BF16)
    mem_copy = remote(mem_own, mem_sib, mem_send, mem_recv, sib, col)
    mem_copy.start()

    get_lq.wait()
    for h in range(heads):
        scores = dot(lq[:, cut(h)], lk[:, cut(h)], NT)
        spread = cum_col[:, h : h + 1] - cum_row[h : h + 1, :]
        weight = jnp.where(causal, jnp.exp(jnp.where(causal, spread, 0.0)), 0.0)
        mixing = (scores * weight).astype(BF16)
        mixed[:, cut(h)] = dot(mixing, lv[:, cut(h)])

    each(n - 1, lambda i: log_copy(i).wait_recv())

    def total(i):
        return jnp.sum(logs[i], axis=1, keepdims=True)

    odd_decay = jnp.exp(total(chip * 2 + 1))
    first = core.astype(F32)
    mem_copy.wait_recv()
    for p in range(half):
        h = core * half + p
        factor = jnp.where(core == 0, odd_decay[p : p + 1], odd_decay[half + p : half + p + 1])
        mine = mem_own[h].astype(F32)
        other = mem_sib[h].astype(F32)
        early = jnp.where(first > 0.5, other, mine)
        late = jnp.where(first > 0.5, mine, other)
        tot_own[p] = (factor * early + late).astype(BF16)

    def tot_copy(i):
        return remote(
            tot_own,
            tot_all.at[chip],
            tot_send.at[i],
            tot_recv.at[chip],
            i * 2 + core,
            col,
        )

    def tot_go(i):
        @pl.when(i > chip)
        def _():
            tot_copy(i).start()

    each(chips, tot_go)

    scale = HEAD_DIM ** (-0.5)
    own_segment = seg_ref[me]
    get_sq.wait()
    for h in range(heads):
        qs[h * tokens : (h + 1) * tokens, :] = sq[:, cut(h)]

    def soft_first():
        logits = dot(qs[...], kv[me, 0], NT) * scale
        shape = (heads, tokens, tokens)
        logits = jnp.where(causal[None], logits.reshape(shape), -1e30).reshape(
            heads * tokens, tokens
        )
        peak = jnp.max(logits, axis=1, keepdims=True)
        weights = jnp.exp(logits - peak)
        top[...] = peak
        den[...] = jnp.sum(weights, axis=1, keepdims=True)
        acc[...] = dot(weights.astype(BF16), kv[me, 1])

    def soft_next(owner):
        shown = seg_ref[owner] < own_segment
        bias = jnp.where(shown, 0.0, -1e30).astype(F32)
        logits = dot(qs[...], kv[owner, 0], NT) * scale + bias
        old = top[...]
        peak = jnp.maximum(old, jnp.max(logits, axis=1, keepdims=True))
        fade = jnp.exp(old - peak)
        weights = jnp.exp(logits - peak)
        top[...] = peak
        den[...] = den[...] * fade + jnp.sum(weights, axis=1, keepdims=True)
        acc[...] = acc[...] * fade + dot(weights.astype(BF16), kv[owner, 1])

    soft_first()

    def fwd_copy(i, part, owner):
        return remote(
            kv.at[owner, part],
            kv.at[owner, part],
            fwd_send.at[i, part],
            kv_recv.at[chips + i, part],
            sib,
            col,
        )

    def kv_pass(i):
        owner = near(i) * 2 + core
        for part in range(2):
            kv_copy(i, part, far(i)).wait_recv()
            fwd_copy(i, part, owner).start()
        soft_next(owner)

    each(chips - 1, kv_pass)

    pre[...] = jnp.zeros_like(pre)

    def join(i):
        @pl.when(i < chip)
        def _():
            remote(tot_own, tot_all.at[i], tot_send.at[i], tot_recv.at[i], sib, col).wait_recv()
            both = jnp.exp(total(i * 2) + total(i * 2 + 1))
            for p in range(half):
                factor = jnp.where(core == 0, both[p : p + 1], both[half + p : half + p + 1])
                pre[p] = factor * pre[p] + tot_all[i, p].astype(F32)

    each(chips, join)
    ent_own[...] = pre[...].astype(BF16)
    ent_copy = remote(ent_own, ent_sib, ent_send, ent_recv, sib, col)
    ent_copy.start()

    kv_copy(chips - 1, 0, sib).wait_recv()
    kv_copy(chips - 1, 1, sib).wait_recv()
    soft_next(sib)

    even_decay = jnp.exp(total(chip * 2))
    ent_copy.wait_recv()
    squares = jnp.zeros((tokens, HEAD_DIM), F32)
    for h in range(heads):
        pair, p = h // half, h % half
        here = jnp.where(core == pair, ent_own[p].astype(F32), ent_sib[p].astype(F32))
        later = even_decay[h : h + 1] * here + mem_sib[h].astype(F32)
        state = jnp.where(core == 0, here, later).astype(BF16)
        lifted = (lq[:, cut(h)].astype(F32) * lift[:, h : h + 1]).astype(BF16)
        value = mixed[:, cut(h)] + dot(lifted, state)
        mixed[:, cut(h)] = value
        squares = squares + value * value
    sums[col] = dot(jnp.ones((8, HEAD_DIM), F32), squares, NT, HIGH)

    def sum_copy(i):
        return remote(
            sums.at[col],
            sums.at[col],
            sum_send.at[i],
            sum_recv.at[i],
            me,
            (col + 1 + i) % nh,
        )

    each(nh - 1, lambda i: sum_copy(i).start())

    def kv_last(i):
        for part in range(2):
            fwd_copy(i, part, near(i) * 2 + core).wait_recv()
        soft_next(near(i) * 2 + 1 - core)

    each(chips - 1, kv_last)
    for h in range(heads):
        r = slice(h * tokens, (h + 1) * tokens)
        soft_ref[:, cut(h)] = (acc[r, :] / den[r, :]).astype(BF16)

    get_gate.wait()
    each(nh - 1, lambda i: sum_copy(i).wait_recv())
    everyone = sums[...].reshape(nh * 8, tokens)
    eighth = jnp.full((nh * 8, HEAD_DIM), 0.125, F32)
    spread_sums = dot(everyone, eighth, TN, HIGH)
    inverse = lax.rsqrt(spread_sums / (heads * HEAD_DIM * nh) + NORM_EPS)
    for h in range(heads):
        opened = jax.nn.sigmoid(gate[:, cut(h)].astype(F32))
        lin_ref[:, cut(h)] = (mixed[:, cut(h)] * inverse * gain_ref[:, cut(h)] * opened).astype(
            BF16
        )

    each(n - 1, lambda i: log_copy(i).wait_send())

    def kv_sent(i):
        for part in range(2):
            kv_copy(i, part, sib).wait_send()

    each(chips, kv_sent)

    def fwd_sent(i):
        for part in range(2):
            fwd_copy(i, part, near(i) * 2 + core).wait_send()

    each(chips - 1, fwd_sent)
    mem_copy.wait_send()

    def tot_sent(i):
        @pl.when(i > chip)
        def _():
            tot_copy(i).wait_send()

    each(chips, tot_sent)
    ent_copy.wait_send()
    each(nh - 1, lambda i: sum_copy(i).wait_send())


def solution(mesh):
    n, nh = mesh.shape["seq"], mesh.shape["head"]
    chips = n // 2

    def step(lq, lk, lv, ld, gate, gain, sq, sk, sv, seg):
        tokens, width = lq.shape
        heads = width // HEAD_DIM
        half = heads // 2
        block = (tokens, width)
        square = (HEAD_DIM, HEAD_DIM)
        dma = pltpu.SemaphoreType.DMA
        anywhere = pl.BlockSpec(memory_space=pl.ANY)
        vmem = pl.BlockSpec(memory_space=pltpu.VMEM)
        return pl.pallas_call(
            functools.partial(kernel, n, nh),
            out_shape=[jax.ShapeDtypeStruct(block, BF16)] * 2,
            in_specs=[anywhere] * 5
            + [vmem]
            + [anywhere] * 3
            + [pl.BlockSpec(memory_space=pltpu.SMEM)],
            out_specs=[vmem, vmem],
            scratch_shapes=[
                pltpu.VMEM(block, BF16),
                pltpu.VMEM(block, BF16),
                pltpu.VMEM(block, BF16),
                pltpu.VMEM(block, BF16),
                pltpu.VMEM(block, BF16),
                pltpu.VMEM((heads * tokens, HEAD_DIM), BF16),
                pltpu.VMEM((n, 2, tokens, HEAD_DIM), BF16),
                pltpu.VMEM((n, heads, tokens), F32),
                pltpu.VMEM((heads,) + square, BF16),
                pltpu.VMEM((heads,) + square, BF16),
                pltpu.VMEM((half,) + square, BF16),
                pltpu.VMEM((chips, half) + square, BF16),
                pltpu.VMEM((half,) + square, F32),
                pltpu.VMEM((half,) + square, BF16),
                pltpu.VMEM((half,) + square, BF16),
                pltpu.VMEM(block, F32),
                pltpu.VMEM((nh, 8, tokens), F32),
                pltpu.VMEM((heads * tokens, 1), F32),
                pltpu.VMEM((heads * tokens, HEAD_DIM), F32),
                pltpu.VMEM((heads * tokens, 1), F32),
                dma((8,)),
                dma((chips, 2)),
                dma((2 * chips, 2)),
                dma((chips, 2)),
                dma((n,)),
                dma((n,)),
                dma,
                dma,
                dma((chips,)),
                dma((chips,)),
                dma,
                dma,
                dma((nh,)),
                dma((nh,)),
            ],
            compiler_params=pltpu.CompilerParams(
                collective_id=0,
                has_side_effects=True,
                vmem_limit_bytes=40 * 1024 * 1024,
            ),
        )(lq, lk, lv, ld, gate, gain.reshape(1, width), sq, sk, sv, seg)

    return jax.shard_map(
        step,
        mesh=mesh,
        in_specs=(
            P("seq", "head"),
            P("seq", "head"),
            P("seq", "head"),
            P("head", "seq"),
            P("seq", "head"),
            P("head"),
            P("seq", "head"),
            P("seq", None),
            P("seq", None),
            P(),
        ),
        out_specs=(P("seq", "head"), P("seq", "head")),
        check_vma=False,
    )
```

```python
import functools

import jax
import jax.numpy as jnp
from jax import lax
from jax.experimental import pallas as pl
from jax.experimental.pallas import tpu as pltpu
from jax.sharding import PartitionSpec as P

HEAD_DIM = 128
Q_PER_KV = 8
NORM_EPS = 1e-06
MESH = pl.DeviceIdType.MESH
F32 = jnp.float32
BF16 = jnp.bfloat16
NT = (((1,), (1,)), ((), ()))
TN = (((0,), (0,)), ((), ()))
HIGH = lax.Precision.HIGHEST


def dot(a, b, dims=(((1,), (0,)), ((), ())), precision=None):
    return lax.dot_general(a, b, dims, preferred_element_type=F32, precision=precision)


def each(count, body):
    if count <= 8:
        for i in range(count):
            body(i)
    else:
        lax.fori_loop(0, count, lambda i, _: (body(i), 0)[1], 0)


def kernel(
    n,
    nh,
    lq_hbm,
    lk_hbm,
    lv_hbm,
    ld_hbm,
    gate_hbm,
    gain_hbm,
    sq_hbm,
    sk_hbm,
    sv_hbm,
    seg_hbm,
    lin_ref,
    soft_ref,
    lq,
    lk,
    lv,
    gate,
    sq,
    qs,
    kv,
    logs,
    mem_own,
    mem_sib,
    tot_own,
    tot_all,
    pre,
    ent_own,
    ent_sib,
    mixed,
    sums,
    top,
    acc,
    den,
    gain_ref,
    seg_ref,
    in_sem,
    kv_send,
    kv_recv,
    fwd_send,
    log_send,
    log_recv,
    mem_send,
    mem_recv,
    tot_send,
    tot_recv,
    ent_send,
    ent_recv,
    sum_send,
    sum_recv,
):
    chips = n // 2
    me = lax.axis_index("seq")
    col = lax.axis_index("head")
    chip, core = me // 2, me % 2
    sib = chip * 2 + 1 - core
    tokens = lq.shape[0]
    heads = lq.shape[1] // HEAD_DIM
    half = heads // 2
    share = pl.multiple_of((col * heads // Q_PER_KV) * HEAD_DIM, HEAD_DIM)

    barrier = pltpu.get_barrier_semaphore()

    def greet(i):
        pl.semaphore_signal(
            barrier, inc=1, device_id=((me + 1 + i) % n, col), device_id_type=MESH
        )

    def greet_col(i):
        pl.semaphore_signal(
            barrier, inc=1, device_id=(me, (col + 1 + i) % nh), device_id_type=MESH
        )

    each(n - 1, greet)
    each(nh - 1, greet_col)

    def local(src, dst, at):
        copy = pltpu.make_async_copy(src, dst, in_sem.at[at])
        copy.start()
        return copy

    get_ld = local(ld_hbm, logs.at[me], 0)
    get_lk = local(lk_hbm, lk, 1)
    get_lv = local(lv_hbm, lv, 2)
    get_lq = local(lq_hbm, lq, 3)
    get_sk = local(sk_hbm.at[:, pl.ds(share, HEAD_DIM)], kv.at[me, 0], 4)
    get_sv = local(sv_hbm.at[:, pl.ds(share, HEAD_DIM)], kv.at[me, 1], 5)
    get_sq = local(sq_hbm, sq, 6)
    get_gate = local(gate_hbm, gate, 7)
    get_gain = local(gain_hbm, gain_ref, 8)
    get_seg = local(seg_hbm, seg_ref, 9)

    def remote(src, dst, send, recv, seq_to, col_to):
        return pltpu.make_async_remote_copy(
            src_ref=src,
            dst_ref=dst,
            send_sem=send,
            recv_sem=recv,
            device_id=(seq_to, col_to),
            device_id_type=MESH,
        )

    get_ld.wait()
    get_sk.wait()
    get_sv.wait()
    pl.semaphore_wait(barrier, n - 1 + nh - 1)

    def log_copy(i):
        return remote(
            logs.at[me],
            logs.at[me],
            log_send.at[i],
            log_recv.at[i],
            (me + 1 + i) % n,
            col,
        )

    def kv_copy(i, part, to):
        return remote(
            kv.at[me, part],
            kv.at[me, part],
            kv_send.at[i, part],
            kv_recv.at[i, part],
            to,
            col,
        )

    def far(i):
        return ((chip + 1 + i) % chips) * 2 + core

    def near(i):
        return (chip + chips - 1 - i) % chips

    each(n - 1, lambda i: log_copy(i).start())

    def kv_go(i):
        kv_copy(i, 0, far(i)).start()
        kv_copy(i, 1, far(i)).start()

    each(chips - 1, kv_go)
    kv_copy(chips - 1, 0, sib).start()
    kv_copy(chips - 1, 1, sib).start()

    rows = lax.broadcasted_iota(jnp.int32, (tokens, tokens), 0)
    cols = lax.broadcasted_iota(jnp.int32, (tokens, tokens), 1)
    causal = rows >= cols
    lower = jnp.where(causal, 1.0, 0.0).astype(F32)
    decay = logs[me]
    cum_row = dot(decay, lower, NT, HIGH)
    cum_col = dot(lower, decay, NT, HIGH)
    tail = jnp.exp(cum_col[tokens - 1 : tokens, :] - cum_col)
    lift = jnp.exp(cum_col)

    def cut(h):
        return slice(h * HEAD_DIM, (h + 1) * HEAD_DIM)

    get_lk.wait()
    get_lv.wait()
    for h in range(heads):
        weighted = (lk[:, cut(h)].astype(F32) * tail[:, h : h + 1]).astype(BF16)
        mem_own[h] = dot(weighted, lv[:, cut(h)], TN).astype(BF16)
    mem_copy = remote(mem_own, mem_sib, mem_send, mem_recv, sib, col)
    mem_copy.start()

    get_lq.wait()
    for h in range(heads):
        scores = dot(lq[:, cut(h)], lk[:, cut(h)], NT)
        spread = cum_col[:, h : h + 1] - cum_row[h : h + 1, :]
        weight = jnp.where(causal, jnp.exp(jnp.where(causal, spread, 0.0)), 0.0)
        mixing = (scores * weight).astype(BF16)
        mixed[:, cut(h)] = dot(mixing, lv[:, cut(h)])

    each(n - 1, lambda i: log_copy(i).wait_recv())

    def total(i):
        return jnp.sum(logs[i], axis=1, keepdims=True)

    odd_decay = jnp.exp(total(chip * 2 + 1))
    first = core.astype(F32)
    mem_copy.wait_recv()
    for p in range(half):
        h = core * half + p
        factor = jnp.where(core == 0, odd_decay[p : p + 1], odd_decay[half + p : half + p + 1])
        mine = mem_own[h].astype(F32)
        other = mem_sib[h].astype(F32)
        early = jnp.where(first > 0.5, other, mine)
        late = jnp.where(first > 0.5, mine, other)
        tot_own[p] = (factor * early + late).astype(BF16)

    def tot_copy(i):
        return remote(
            tot_own,
            tot_all.at[chip],
            tot_send.at[i],
            tot_recv.at[chip],
            i * 2 + core,
            col,
        )

    def tot_go(i):
        @pl.when(i > chip)
        def _():
            tot_copy(i).start()

    each(chips, tot_go)

    scale = HEAD_DIM ** (-0.5)
    get_seg.wait()
    own_segment = seg_ref[me]
    get_sq.wait()
    for h in range(heads):
        qs[h * tokens : (h + 1) * tokens, :] = sq[:, cut(h)]

    def soft_first():
        logits = dot(qs[...], kv[me, 0], NT) * scale
        shape = (heads, tokens, tokens)
        logits = jnp.where(causal[None], logits.reshape(shape), -1e30).reshape(
            heads * tokens, tokens
        )
        peak = jnp.max(logits, axis=1, keepdims=True)
        weights = jnp.exp(logits - peak)
        top[...] = peak
        den[...] = jnp.sum(weights, axis=1, keepdims=True)
        acc[...] = dot(weights.astype(BF16), kv[me, 1])

    def soft_next(owner):
        shown = seg_ref[owner] < own_segment
        bias = jnp.where(shown, 0.0, -1e30).astype(F32)
        logits = dot(qs[...], kv[owner, 0], NT) * scale + bias
        old = top[...]
        peak = jnp.maximum(old, jnp.max(logits, axis=1, keepdims=True))
        fade = jnp.exp(old - peak)
        weights = jnp.exp(logits - peak)
        top[...] = peak
        den[...] = den[...] * fade + jnp.sum(weights, axis=1, keepdims=True)
        acc[...] = acc[...] * fade + dot(weights.astype(BF16), kv[owner, 1])

    soft_first()

    def fwd_copy(i, part, owner):
        return remote(
            kv.at[owner, part],
            kv.at[owner, part],
            fwd_send.at[i, part],
            kv_recv.at[chips + i, part],
            sib,
            col,
        )

    def kv_pass(i):
        owner = near(i) * 2 + core
        for part in range(2):
            kv_copy(i, part, far(i)).wait_recv()
            fwd_copy(i, part, owner).start()
        soft_next(owner)

    each(chips - 1, kv_pass)

    pre[...] = jnp.zeros_like(pre)

    def join(i):
        @pl.when(i < chip)
        def _():
            remote(tot_own, tot_all.at[i], tot_send.at[i], tot_recv.at[i], sib, col).wait_recv()
            both = jnp.exp(total(i * 2) + total(i * 2 + 1))
            for p in range(half):
                factor = jnp.where(core == 0, both[p : p + 1], both[half + p : half + p + 1])
                pre[p] = factor * pre[p] + tot_all[i, p].astype(F32)

    each(chips, join)
    ent_own[...] = pre[...].astype(BF16)
    ent_copy = remote(ent_own, ent_sib, ent_send, ent_recv, sib, col)
    ent_copy.start()

    kv_copy(chips - 1, 0, sib).wait_recv()
    kv_copy(chips - 1, 1, sib).wait_recv()
    soft_next(sib)

    even_decay = jnp.exp(total(chip * 2))
    ent_copy.wait_recv()
    squares = jnp.zeros((tokens, HEAD_DIM), F32)
    for h in range(heads):
        pair, p = h // half, h % half
        here = jnp.where(core == pair, ent_own[p].astype(F32), ent_sib[p].astype(F32))
        later = even_decay[h : h + 1] * here + mem_sib[h].astype(F32)
        state = jnp.where(core == 0, here, later).astype(BF16)
        lifted = (lq[:, cut(h)].astype(F32) * lift[:, h : h + 1]).astype(BF16)
        value = mixed[:, cut(h)] + dot(lifted, state)
        mixed[:, cut(h)] = value
        squares = squares + value * value
    sums[col] = dot(jnp.ones((8, HEAD_DIM), F32), squares, NT, HIGH)

    def sum_copy(i):
        return remote(
            sums.at[col],
            sums.at[col],
            sum_send.at[i],
            sum_recv.at[i],
            me,
            (col + 1 + i) % nh,
        )

    each(nh - 1, lambda i: sum_copy(i).start())

    def kv_last(i):
        for part in range(2):
            fwd_copy(i, part, near(i) * 2 + core).wait_recv()
        soft_next(near(i) * 2 + 1 - core)

    each(chips - 1, kv_last)
    for h in range(heads):
        r = slice(h * tokens, (h + 1) * tokens)
        sq[:, cut(h)] = (acc[r, :] / den[r, :]).astype(BF16)
    put_soft = local(sq, soft_ref, 10)

    get_gate.wait()
    get_gain.wait()
    each(nh - 1, lambda i: sum_copy(i).wait_recv())
    everyone = sums[...].reshape(nh * 8, tokens)
    eighth = jnp.full((nh * 8, HEAD_DIM), 0.125, F32)
    spread_sums = dot(everyone, eighth, TN, HIGH)
    inverse = lax.rsqrt(spread_sums / (heads * HEAD_DIM * nh) + NORM_EPS)
    for h in range(heads):
        opened = jax.nn.sigmoid(gate[:, cut(h)].astype(F32))
        lq[:, cut(h)] = (mixed[:, cut(h)] * inverse * gain_ref[:, cut(h)] * opened).astype(
            BF16
        )

    put_lin = local(lq, lin_ref, 11)

    each(n - 1, lambda i: log_copy(i).wait_send())

    def kv_sent(i):
        for part in range(2):
            kv_copy(i, part, sib).wait_send()

    each(chips, kv_sent)

    def fwd_sent(i):
        for part in range(2):
            fwd_copy(i, part, near(i) * 2 + core).wait_send()

    each(chips - 1, fwd_sent)
    mem_copy.wait_send()

    def tot_sent(i):
        @pl.when(i > chip)
        def _():
            tot_copy(i).wait_send()

    each(chips, tot_sent)
    ent_copy.wait_send()
    each(nh - 1, lambda i: sum_copy(i).wait_send())
    put_soft.wait()
    put_lin.wait()


def deliver(lin_in, soft_in, lin_out, soft_out, sem):
    first = pltpu.make_async_copy(lin_in, lin_out, sem.at[0])
    second = pltpu.make_async_copy(soft_in, soft_out, sem.at[1])
    first.start()
    second.start()
    first.wait()
    second.wait()


def solution(mesh):
    n, nh = mesh.shape["seq"], mesh.shape["head"]
    chips = n // 2

    def step(lq, lk, lv, ld, gate, gain, sq, sk, sv, seg):
        tokens, width = lq.shape
        heads = width // HEAD_DIM
        half = heads // 2
        block = (tokens, width)
        square = (HEAD_DIM, HEAD_DIM)
        dma = pltpu.SemaphoreType.DMA
        anywhere = pl.BlockSpec(memory_space=pltpu.HBM)
        results = pl.pallas_call(
            functools.partial(kernel, n, nh),
            out_shape=[jax.ShapeDtypeStruct(block, BF16)] * 2,
            in_specs=[anywhere] * 10,
            out_specs=[anywhere] * 2,
            scratch_shapes=[
                pltpu.VMEM(block, BF16),
                pltpu.VMEM(block, BF16),
                pltpu.VMEM(block, BF16),
                pltpu.VMEM(block, BF16),
                pltpu.VMEM(block, BF16),
                pltpu.VMEM((heads * tokens, HEAD_DIM), BF16),
                pltpu.VMEM((n, 2, tokens, HEAD_DIM), BF16),
                pltpu.VMEM((n, heads, tokens), F32),
                pltpu.VMEM((heads,) + square, BF16),
                pltpu.VMEM((heads,) + square, BF16),
                pltpu.VMEM((half,) + square, BF16),
                pltpu.VMEM((chips, half) + square, BF16),
                pltpu.VMEM((half,) + square, F32),
                pltpu.VMEM((half,) + square, BF16),
                pltpu.VMEM((half,) + square, BF16),
                pltpu.VMEM(block, F32),
                pltpu.VMEM((nh, 8, tokens), F32),
                pltpu.VMEM((heads * tokens, 1), F32),
                pltpu.VMEM((heads * tokens, HEAD_DIM), F32),
                pltpu.VMEM((heads * tokens, 1), F32),
                pltpu.VMEM((1, width), F32),
                pltpu.SMEM((n,), jnp.int32),
                dma((12,)),
                dma((chips, 2)),
                dma((2 * chips, 2)),
                dma((chips, 2)),
                dma((n,)),
                dma((n,)),
                dma,
                dma,
                dma((chips,)),
                dma((chips,)),
                dma,
                dma,
                dma((nh,)),
                dma((nh,)),
            ],
            compiler_params=pltpu.CompilerParams(
                collective_id=0,
                has_side_effects=True,
                vmem_limit_bytes=63 * 1024 * 1024,
            ),
        )(lq, lk, lv, ld, gate, gain.reshape(1, width), sq, sk, sv, seg)
        return pl.pallas_call(
            deliver,
            out_shape=[jax.ShapeDtypeStruct(block, BF16)] * 2,
            in_specs=[anywhere] * 2,
            out_specs=[anywhere] * 2,
            scratch_shapes=[dma((2,))],
        )(*results)

    return jax.shard_map(
        step,
        mesh=mesh,
        in_specs=(
            P("seq", "head"),
            P("seq", "head"),
            P("seq", "head"),
            P("head", "seq"),
            P("seq", "head"),
            P("head"),
            P("seq", "head"),
            P("seq", None),
            P("seq", None),
            P(),
        ),
        out_specs=(P("seq", "head"), P("seq", "head")),
        check_vma=False,
    )
```

```python
import functools

import jax
import jax.numpy as jnp
from jax import lax
from jax.experimental import pallas as pl
from jax.experimental.pallas import tpu as pltpu
from jax.sharding import PartitionSpec as P

HEAD_DIM = 128
Q_PER_KV = 8
NORM_EPS = 1e-06
MESH = pl.DeviceIdType.MESH
F32 = jnp.float32
BF16 = jnp.bfloat16
NT = (((1,), (1,)), ((), ()))
TN = (((0,), (0,)), ((), ()))
HIGH = lax.Precision.HIGHEST


def dot(a, b, dims=(((1,), (0,)), ((), ())), precision=None):
    return lax.dot_general(a, b, dims, preferred_element_type=F32, precision=precision)


def each(count, body):
    if count <= 8:
        for i in range(count):
            body(i)
    else:
        lax.fori_loop(0, count, lambda i, _: (body(i), 0)[1], 0)


def kernel(
    n,
    nh,
    lq_hbm,
    lk_hbm,
    lv_hbm,
    ld_hbm,
    gate_hbm,
    gain_hbm,
    sq_hbm,
    sk_hbm,
    sv_hbm,
    seg_hbm,
    lin_ref,
    soft_ref,
    lq,
    lk,
    lv,
    gate,
    sq,
    qs,
    kv,
    logs,
    mem_own,
    mem_sib,
    tot_own,
    tot_all,
    pre,
    ent_own,
    ent_sib,
    mixed,
    sums,
    top,
    acc,
    den,
    gain_ref,
    seg_ref,
    in_sem,
    kv_send,
    kv_recv,
    fwd_send,
    log_send,
    log_recv,
    mem_send,
    mem_recv,
    tot_send,
    tot_recv,
    ent_send,
    ent_recv,
    sum_send,
    sum_recv,
):
    chips = n // 2
    me = lax.axis_index("seq")
    col = lax.axis_index("head")
    chip, core = me // 2, me % 2
    sib = chip * 2 + 1 - core
    tokens = lq.shape[0]
    heads = lq.shape[1] // HEAD_DIM
    half = heads // 2
    share = pl.multiple_of((col * heads // Q_PER_KV) * HEAD_DIM, HEAD_DIM)

    barrier = pltpu.get_barrier_semaphore()

    def greet(i):
        pl.semaphore_signal(
            barrier, inc=1, device_id=((me + 1 + i) % n, col), device_id_type=MESH
        )

    def greet_col(i):
        pl.semaphore_signal(
            barrier, inc=1, device_id=(me, (col + 1 + i) % nh), device_id_type=MESH
        )

    each(n - 1, greet)
    each(nh - 1, greet_col)

    def local(src, dst, at):
        copy = pltpu.make_async_copy(src, dst, in_sem.at[at])
        copy.start()
        return copy

    get_ld = local(ld_hbm, logs.at[me], 0)
    get_lk = local(lk_hbm, lk, 1)
    get_lv = local(lv_hbm, lv, 2)
    get_lq = local(lq_hbm, lq, 3)
    get_sk = local(sk_hbm.at[:, pl.ds(share, HEAD_DIM)], kv.at[me, 0], 4)
    get_sv = local(sv_hbm.at[:, pl.ds(share, HEAD_DIM)], kv.at[me, 1], 5)
    get_sq = local(sq_hbm, sq, 6)
    get_gate = local(gate_hbm, gate, 7)
    get_gain = local(gain_hbm, gain_ref, 8)
    get_seg = local(seg_hbm, seg_ref, 9)

    def remote(src, dst, send, recv, seq_to, col_to):
        return pltpu.make_async_remote_copy(
            src_ref=src,
            dst_ref=dst,
            send_sem=send,
            recv_sem=recv,
            device_id=(seq_to, col_to),
            device_id_type=MESH,
        )

    get_ld.wait()
    get_sk.wait()
    get_sv.wait()
    pl.semaphore_wait(barrier, n - 1 + nh - 1)

    def log_copy(i):
        return remote(
            logs.at[me],
            logs.at[me],
            log_send.at[i],
            log_recv.at[i],
            (me + 1 + i) % n,
            col,
        )

    def kv_copy(i, part, to):
        return remote(
            kv.at[me, part],
            kv.at[me, part],
            kv_send.at[i, part],
            kv_recv.at[i, part],
            to,
            col,
        )

    def far(i):
        return ((chip + 1 + i) % chips) * 2 + core

    def near(i):
        return (chip + chips - 1 - i) % chips

    each(n - 1, lambda i: log_copy(i).start())

    def kv_go(i):
        kv_copy(i, 0, far(i)).start()
        kv_copy(i, 1, far(i)).start()

    each(chips - 1, kv_go)
    kv_copy(chips - 1, 0, sib).start()
    kv_copy(chips - 1, 1, sib).start()

    rows = lax.broadcasted_iota(jnp.int32, (tokens, tokens), 0)
    cols = lax.broadcasted_iota(jnp.int32, (tokens, tokens), 1)
    causal = rows >= cols
    lower = jnp.where(causal, 1.0, 0.0).astype(F32)
    decay = logs[me]
    cum_row = dot(decay, lower, NT, HIGH)
    cum_col = dot(lower, decay, NT, HIGH)
    tail = jnp.exp(cum_col[tokens - 1 : tokens, :] - cum_col)
    lift = jnp.exp(cum_col)

    def cut(h):
        return slice(h * HEAD_DIM, (h + 1) * HEAD_DIM)

    get_lk.wait()
    get_lv.wait()
    for h in range(heads):
        weighted = (lk[:, cut(h)].astype(F32) * tail[:, h : h + 1]).astype(BF16)
        mem_own[h] = dot(weighted, lv[:, cut(h)], TN).astype(BF16)
    mem_copy = remote(mem_own, mem_sib, mem_send, mem_recv, sib, col)
    mem_copy.start()

    get_lq.wait()
    for h in range(heads):
        scores = dot(lq[:, cut(h)], lk[:, cut(h)], NT)
        spread = cum_col[:, h : h + 1] - cum_row[h : h + 1, :]
        weight = jnp.where(causal, jnp.exp(jnp.where(causal, spread, 0.0)), 0.0)
        mixing = (scores * weight).astype(BF16)
        mixed[:, cut(h)] = dot(mixing, lv[:, cut(h)])

    each(n - 1, lambda i: log_copy(i).wait_recv())

    def total(i):
        return jnp.sum(logs[i], axis=1, keepdims=True)

    odd_decay = jnp.exp(total(chip * 2 + 1))
    first = core.astype(F32)
    mem_copy.wait_recv()
    for p in range(half):
        h = core * half + p
        factor = jnp.where(core == 0, odd_decay[p : p + 1], odd_decay[half + p : half + p + 1])
        mine = mem_own[h].astype(F32)
        other = mem_sib[h].astype(F32)
        early = jnp.where(first > 0.5, other, mine)
        late = jnp.where(first > 0.5, mine, other)
        tot_own[p] = (factor * early + late).astype(BF16)

    def tot_copy(i):
        return remote(
            tot_own,
            tot_all.at[chip],
            tot_send.at[i],
            tot_recv.at[chip],
            i * 2 + core,
            col,
        )

    def tot_go(i):
        @pl.when(i > chip)
        def _():
            tot_copy(i).start()

    each(chips, tot_go)

    scale = HEAD_DIM ** (-0.5)
    get_seg.wait()
    own_segment = seg_ref[me]
    get_sq.wait()
    for h in range(heads):
        qs[h * tokens : (h + 1) * tokens, :] = sq[:, cut(h)]

    def soft_first():
        logits = dot(qs[...], kv[me, 0], NT) * scale
        shape = (heads, tokens, tokens)
        logits = jnp.where(causal[None], logits.reshape(shape), -1e30).reshape(
            heads * tokens, tokens
        )
        peak = jnp.max(logits, axis=1, keepdims=True)
        weights = jnp.exp(logits - peak)
        top[...] = peak
        den[...] = jnp.sum(weights, axis=1, keepdims=True)
        acc[...] = dot(weights.astype(BF16), kv[me, 1])

    def soft_next(owner):
        shown = seg_ref[owner] < own_segment
        bias = jnp.where(shown, 0.0, -1e30).astype(F32)
        logits = dot(qs[...], kv[owner, 0], NT) * scale + bias
        old = top[...]
        peak = jnp.maximum(old, jnp.max(logits, axis=1, keepdims=True))
        fade = jnp.exp(old - peak)
        weights = jnp.exp(logits - peak)
        top[...] = peak
        den[...] = den[...] * fade + jnp.sum(weights, axis=1, keepdims=True)
        acc[...] = acc[...] * fade + dot(weights.astype(BF16), kv[owner, 1])

    soft_first()

    def fwd_copy(i, part, owner):
        return remote(
            kv.at[owner, part],
            kv.at[owner, part],
            fwd_send.at[i, part],
            kv_recv.at[chips + i, part],
            sib,
            col,
        )

    def kv_pass(i):
        owner = near(i) * 2 + core
        for part in range(2):
            kv_copy(i, part, far(i)).wait_recv()
            fwd_copy(i, part, owner).start()
        soft_next(owner)

    each(chips - 1, kv_pass)

    pre[...] = jnp.zeros_like(pre)

    def join(i):
        @pl.when(i < chip)
        def _():
            remote(tot_own, tot_all.at[i], tot_send.at[i], tot_recv.at[i], sib, col).wait_recv()
            both = jnp.exp(total(i * 2) + total(i * 2 + 1))
            for p in range(half):
                factor = jnp.where(core == 0, both[p : p + 1], both[half + p : half + p + 1])
                pre[p] = factor * pre[p] + tot_all[i, p].astype(F32)

    each(chips, join)
    ent_own[...] = pre[...].astype(BF16)
    ent_copy = remote(ent_own, ent_sib, ent_send, ent_recv, sib, col)
    ent_copy.start()

    kv_copy(chips - 1, 0, sib).wait_recv()
    kv_copy(chips - 1, 1, sib).wait_recv()
    soft_next(sib)

    even_decay = jnp.exp(total(chip * 2))
    ent_copy.wait_recv()
    squares = jnp.zeros((tokens, HEAD_DIM), F32)
    for h in range(heads):
        pair, p = h // half, h % half
        here = jnp.where(core == pair, ent_own[p].astype(F32), ent_sib[p].astype(F32))
        later = even_decay[h : h + 1] * here + mem_sib[h].astype(F32)
        state = jnp.where(core == 0, here, later).astype(BF16)
        lifted = (lq[:, cut(h)].astype(F32) * lift[:, h : h + 1]).astype(BF16)
        value = mixed[:, cut(h)] + dot(lifted, state)
        mixed[:, cut(h)] = value
        squares = squares + value * value
    sums[col] = dot(jnp.ones((8, HEAD_DIM), F32), squares, NT, HIGH)

    def sum_copy(i):
        return remote(
            sums.at[col],
            sums.at[col],
            sum_send.at[i],
            sum_recv.at[i],
            me,
            (col + 1 + i) % nh,
        )

    each(nh - 1, lambda i: sum_copy(i).start())

    def kv_last(i):
        for part in range(2):
            fwd_copy(i, part, near(i) * 2 + core).wait_recv()
        soft_next(near(i) * 2 + 1 - core)

    each(chips - 1, kv_last)
    for h in range(heads):
        r = slice(h * tokens, (h + 1) * tokens)
        soft_ref[:, cut(h)] = (acc[r, :] / den[r, :]).astype(BF16)

    get_gate.wait()
    get_gain.wait()
    each(nh - 1, lambda i: sum_copy(i).wait_recv())
    everyone = sums[...].reshape(nh * 8, tokens)
    eighth = jnp.full((nh * 8, HEAD_DIM), 0.125, F32)
    spread_sums = dot(everyone, eighth, TN, HIGH)
    inverse = lax.rsqrt(spread_sums / (heads * HEAD_DIM * nh) + NORM_EPS)
    for h in range(heads):
        opened = jax.nn.sigmoid(gate[:, cut(h)].astype(F32))
        lin_ref[:, cut(h)] = (mixed[:, cut(h)] * inverse * gain_ref[:, cut(h)] * opened).astype(
            BF16
        )

    each(n - 1, lambda i: log_copy(i).wait_send())

    def kv_sent(i):
        for part in range(2):
            kv_copy(i, part, sib).wait_send()

    each(chips, kv_sent)

    def fwd_sent(i):
        for part in range(2):
            fwd_copy(i, part, near(i) * 2 + core).wait_send()

    each(chips - 1, fwd_sent)
    mem_copy.wait_send()

    def tot_sent(i):
        @pl.when(i > chip)
        def _():
            tot_copy(i).wait_send()

    each(chips, tot_sent)
    ent_copy.wait_send()
    each(nh - 1, lambda i: sum_copy(i).wait_send())


def solution(mesh):
    n, nh = mesh.shape["seq"], mesh.shape["head"]
    chips = n // 2

    def step(lq, lk, lv, ld, gate, gain, sq, sk, sv, seg):
        tokens, width = lq.shape
        heads = width // HEAD_DIM
        half = heads // 2
        block = (tokens, width)
        square = (HEAD_DIM, HEAD_DIM)
        dma = pltpu.SemaphoreType.DMA
        anywhere = pl.BlockSpec(memory_space=pltpu.HBM)
        operands = [
            pltpu.with_memory_space_constraint(a, pltpu.HBM)
            for a in (lq, lk, lv, ld, gate, gain.reshape(1, width), sq, sk, sv, seg)
        ]
        results = pl.pallas_call(
            functools.partial(kernel, n, nh),
            out_shape=[jax.ShapeDtypeStruct(block, BF16)] * 2,
            in_specs=[anywhere] * 10,
            out_specs=[pl.BlockSpec(memory_space=pltpu.VMEM)] * 2,
            scratch_shapes=[
                pltpu.VMEM(block, BF16),
                pltpu.VMEM(block, BF16),
                pltpu.VMEM(block, BF16),
                pltpu.VMEM(block, BF16),
                pltpu.VMEM(block, BF16),
                pltpu.VMEM((heads * tokens, HEAD_DIM), BF16),
                pltpu.VMEM((n, 2, tokens, HEAD_DIM), BF16),
                pltpu.VMEM((n, heads, tokens), F32),
                pltpu.VMEM((heads,) + square, BF16),
                pltpu.VMEM((heads,) + square, BF16),
                pltpu.VMEM((half,) + square, BF16),
                pltpu.VMEM((chips, half) + square, BF16),
                pltpu.VMEM((half,) + square, F32),
                pltpu.VMEM((half,) + square, BF16),
                pltpu.VMEM((half,) + square, BF16),
                pltpu.VMEM(block, F32),
                pltpu.VMEM((nh, 8, tokens), F32),
                pltpu.VMEM((heads * tokens, 1), F32),
                pltpu.VMEM((heads * tokens, HEAD_DIM), F32),
                pltpu.VMEM((heads * tokens, 1), F32),
                pltpu.VMEM((1, width), F32),
                pltpu.SMEM((n,), jnp.int32),
                dma((10,)),
                dma((chips, 2)),
                dma((2 * chips, 2)),
                dma((chips, 2)),
                dma((n,)),
                dma((n,)),
                dma,
                dma,
                dma((chips,)),
                dma((chips,)),
                dma,
                dma,
                dma((nh,)),
                dma((nh,)),
            ],
            compiler_params=pltpu.CompilerParams(
                collective_id=0,
                has_side_effects=True,
                vmem_limit_bytes=40 * 1024 * 1024,
            ),
        )(*operands)
        return tuple(results)

    return jax.shard_map(
        step,
        mesh=mesh,
        in_specs=(
            P("seq", "head"),
            P("seq", "head"),
            P("seq", "head"),
            P("head", "seq"),
            P("seq", "head"),
            P("head"),
            P("seq", "head"),
            P("seq", None),
            P("seq", None),
            P(),
        ),
        out_specs=(P("seq", "head"), P("seq", "head")),
        check_vma=False,
    )
```

```python
import functools

import jax
import jax.numpy as jnp
from jax import lax
from jax.experimental import pallas as pl
from jax.experimental.pallas import tpu as pltpu
from jax.sharding import PartitionSpec as P

HEAD_DIM = 128
Q_PER_KV = 8
NORM_EPS = 1e-06
LOG2E = 1.4426950408889634
MESH = pl.DeviceIdType.MESH
F32 = jnp.float32
BF16 = jnp.bfloat16
NT = (((1,), (1,)), ((), ()))
TN = (((0,), (0,)), ((), ()))
HIGH = lax.Precision.HIGHEST


def dot(a, b, dims=(((1,), (0,)), ((), ())), precision=None):
    return lax.dot_general(a, b, dims, preferred_element_type=F32, precision=precision)


def each(count, body):
    if count <= 8:
        for i in range(count):
            body(i)
    else:
        lax.fori_loop(0, count, lambda i, _: (body(i), 0)[1], 0)


def kernel(
    n,
    nh,
    lq_hbm,
    lk_hbm,
    lv_hbm,
    ld_hbm,
    gate_hbm,
    gain_hbm,
    sq_hbm,
    sk_hbm,
    sv_hbm,
    seg_hbm,
    lin_ref,
    soft_ref,
    lq,
    lk,
    lv,
    gate,
    sq,
    qs,
    kv,
    logs,
    mem_own,
    mem_sib,
    tot_own,
    tot_all,
    pre,
    ent_own,
    ent_sib,
    mixed,
    sums,
    top,
    acc,
    den,
    gain_ref,
    seg_ref,
    in_sem,
    kv_send,
    kv_recv,
    fwd_send,
    log_send,
    log_recv,
    mem_send,
    mem_recv,
    tot_send,
    tot_recv,
    ent_send,
    ent_recv,
    sum_send,
    sum_recv,
):
    chips = n // 2
    me = lax.axis_index("seq")
    col = lax.axis_index("head")
    chip, core = me // 2, me % 2
    sib = chip * 2 + 1 - core
    tokens = lq.shape[0]
    heads = lq.shape[1] // HEAD_DIM
    half = heads // 2
    share = pl.multiple_of((col * heads // Q_PER_KV) * HEAD_DIM, HEAD_DIM)

    barrier = pltpu.get_barrier_semaphore()

    def greet(i):
        pl.semaphore_signal(
            barrier, inc=1, device_id=((me + 1 + i) % n, col), device_id_type=MESH
        )

    def greet_col(i):
        pl.semaphore_signal(
            barrier, inc=1, device_id=(me, (col + 1 + i) % nh), device_id_type=MESH
        )

    each(n - 1, greet)
    each(nh - 1, greet_col)

    def local(src, dst, at):
        copy = pltpu.make_async_copy(src, dst, in_sem.at[at])
        copy.start()
        return copy

    get_ld = local(ld_hbm, logs.at[me], 0)
    get_lk = local(lk_hbm, lk, 1)
    get_lv = local(lv_hbm, lv, 2)
    get_lq = local(lq_hbm, lq, 3)
    get_sk = local(sk_hbm.at[:, pl.ds(share, HEAD_DIM)], kv.at[me, 0], 4)
    get_sv = local(sv_hbm.at[:, pl.ds(share, HEAD_DIM)], kv.at[me, 1], 5)
    get_sq = local(sq_hbm, sq, 6)
    get_gate = local(gate_hbm, gate, 7)
    get_gain = local(gain_hbm, gain_ref, 8)
    get_seg = local(seg_hbm, seg_ref, 9)

    def remote(src, dst, send, recv, seq_to, col_to):
        return pltpu.make_async_remote_copy(
            src_ref=src,
            dst_ref=dst,
            send_sem=send,
            recv_sem=recv,
            device_id=(seq_to, col_to),
            device_id_type=MESH,
        )

    get_ld.wait()
    rows = lax.broadcasted_iota(jnp.int32, (tokens, tokens), 0)
    cols = lax.broadcasted_iota(jnp.int32, (tokens, tokens), 1)
    causal = rows >= cols
    lower = jnp.where(causal, 1.0, 0.0).astype(F32)
    decay = logs[me]
    cum_row = dot(decay, lower, NT, HIGH)
    cum_col = dot(lower, decay, NT, HIGH)
    tail = jnp.exp(cum_col[tokens - 1 : tokens, :] - cum_col)
    lift = jnp.exp(cum_col)

    get_sk.wait()
    get_sv.wait()
    pl.semaphore_wait(barrier, n - 1 + nh - 1)

    def log_copy(i):
        return remote(
            logs.at[me],
            logs.at[me],
            log_send.at[i],
            log_recv.at[i],
            (me + 1 + i) % n,
            col,
        )

    def kv_copy(i, part, to):
        return remote(
            kv.at[me, part],
            kv.at[me, part],
            kv_send.at[i, part],
            kv_recv.at[i, part],
            to,
            col,
        )

    def far(i):
        return ((chip + 1 + i) % chips) * 2 + core

    def near(i):
        return (chip + chips - 1 - i) % chips

    each(n - 1, lambda i: log_copy(i).start())

    def kv_go(i):
        kv_copy(i, 0, far(i)).start()
        kv_copy(i, 1, far(i)).start()

    each(chips - 1, kv_go)
    kv_copy(chips - 1, 0, sib).start()
    kv_copy(chips - 1, 1, sib).start()

    def cut(h):
        return slice(h * HEAD_DIM, (h + 1) * HEAD_DIM)

    get_lk.wait()
    get_lv.wait()
    for h in range(heads):
        weighted = (lk[:, cut(h)].astype(F32) * tail[:, h : h + 1]).astype(BF16)
        mem_own[h] = dot(weighted, lv[:, cut(h)], TN).astype(BF16)
    mem_copy = remote(mem_own, mem_sib, mem_send, mem_recv, sib, col)
    mem_copy.start()

    get_lq.wait()
    for h in range(heads):
        scores = dot(lq[:, cut(h)], lk[:, cut(h)], NT)
        spread = cum_col[:, h : h + 1] - cum_row[h : h + 1, :]
        weight = jnp.where(causal, jnp.exp(jnp.where(causal, spread, 0.0)), 0.0)
        mixing = (scores * weight).astype(BF16)
        mixed[:, cut(h)] = dot(mixing, lv[:, cut(h)])

    each(n - 1, lambda i: log_copy(i).wait_recv())

    def total(i):
        return jnp.sum(logs[i], axis=1, keepdims=True)

    odd_decay = jnp.exp(total(chip * 2 + 1))
    first = core.astype(F32)
    mem_copy.wait_recv()
    for p in range(half):
        h = core * half + p
        factor = jnp.where(core == 0, odd_decay[p : p + 1], odd_decay[half + p : half + p + 1])
        mine = mem_own[h].astype(F32)
        other = mem_sib[h].astype(F32)
        early = jnp.where(first > 0.5, other, mine)
        late = jnp.where(first > 0.5, mine, other)
        tot_own[p] = (factor * early + late).astype(BF16)

    def tot_copy(i):
        return remote(
            tot_own,
            tot_all.at[chip],
            tot_send.at[i],
            tot_recv.at[chip],
            i * 2 + core,
            col,
        )

    def tot_go(i):
        @pl.when(i > chip)
        def _():
            tot_copy(i).start()

    each(chips, tot_go)

    scale = HEAD_DIM ** (-0.5) * LOG2E
    get_seg.wait()
    own_segment = seg_ref[me]
    get_sq.wait()
    for h in range(heads):
        qs[h * tokens : (h + 1) * tokens, :] = sq[:, cut(h)]
    ones = jnp.ones((tokens, HEAD_DIM), BF16)

    def soft_group(owners, first=False):
        keys = jnp.concatenate([kv[o, 0] for o in owners], axis=0)
        values = jnp.concatenate(
            [jnp.concatenate([kv[o, 1], ones], axis=1) for o in owners], axis=0
        )
        raw = dot(qs[...], keys, NT)
        logits = []
        for j, owner in enumerate(owners):
            part = raw[:, j * tokens : (j + 1) * tokens] * scale
            if first and j == 0:
                shape = (heads, tokens, tokens)
                part = jnp.where(causal[None], part.reshape(shape), -1e30)
                part = part.reshape(heads * tokens, tokens)
            else:
                shown = seg_ref[owner] < own_segment
                part = part + jnp.where(shown, 0.0, -1e30).astype(F32)
            logits.append(part)
        peak = jnp.max(functools.reduce(jnp.maximum, logits), axis=1, keepdims=True)
        peak = jnp.broadcast_to(peak, (heads * tokens, HEAD_DIM))
        if not first:
            old = top[...]
            peak = jnp.maximum(old, peak)
            fade = jnp.exp2(old - peak)
        weights = [jnp.exp2(part - peak).astype(BF16) for part in logits]
        both = dot(jnp.concatenate(weights, axis=1), values)
        top[...] = peak
        if first:
            acc[...] = both[:, :HEAD_DIM]
            den[...] = both[:, HEAD_DIM:]
        else:
            acc[...] = acc[...] * fade + both[:, :HEAD_DIM]
            den[...] = den[...] * fade + both[:, HEAD_DIM:]

    def soft_rest(other):
        if chips <= 5:
            soft_group([near(i) * 2 + other for i in range(chips - 1)])
        else:
            each(chips - 1, lambda i: soft_group([near(i) * 2 + other]))

    kv_copy(chips - 1, 0, sib).wait_recv()
    kv_copy(chips - 1, 1, sib).wait_recv()
    soft_group([me, sib], True)

    def fwd_copy(i, part, owner):
        return remote(
            kv.at[owner, part],
            kv.at[owner, part],
            fwd_send.at[i, part],
            kv_recv.at[chips + i, part],
            sib,
            col,
        )

    def kv_pass(i):
        for part in range(2):
            kv_copy(i, part, far(i)).wait_recv()
            fwd_copy(i, part, near(i) * 2 + core).start()

    each(chips - 1, kv_pass)

    pre[...] = jnp.zeros_like(pre)

    def join(i):
        @pl.when(i < chip)
        def _():
            remote(tot_own, tot_all.at[i], tot_send.at[i], tot_recv.at[i], sib, col).wait_recv()
            both = jnp.exp(total(i * 2) + total(i * 2 + 1))
            for p in range(half):
                factor = jnp.where(core == 0, both[p : p + 1], both[half + p : half + p + 1])
                pre[p] = factor * pre[p] + tot_all[i, p].astype(F32)

    each(chips, join)
    ent_own[...] = pre[...].astype(BF16)
    ent_copy = remote(ent_own, ent_sib, ent_send, ent_recv, sib, col)
    ent_copy.start()

    soft_rest(core)

    even_decay = jnp.exp(total(chip * 2))
    ent_copy.wait_recv()
    squares = jnp.zeros((tokens, HEAD_DIM), F32)
    for h in range(heads):
        pair, p = h // half, h % half
        here = jnp.where(core == pair, ent_own[p].astype(F32), ent_sib[p].astype(F32))
        later = even_decay[h : h + 1] * here + mem_sib[h].astype(F32)
        state = jnp.where(core == 0, here, later).astype(BF16)
        lifted = (lq[:, cut(h)].astype(F32) * lift[:, h : h + 1]).astype(BF16)
        value = mixed[:, cut(h)] + dot(lifted, state)
        mixed[:, cut(h)] = value
        squares = squares + value * value
    sums[col] = dot(jnp.ones((8, HEAD_DIM), F32), squares, NT, HIGH)

    def sum_copy(i):
        return remote(
            sums.at[col],
            sums.at[col],
            sum_send.at[i],
            sum_recv.at[i],
            me,
            (col + 1 + i) % nh,
        )

    each(nh - 1, lambda i: sum_copy(i).start())

    def kv_last(i):
        for part in range(2):
            fwd_copy(i, part, near(i) * 2 + core).wait_recv()

    each(chips - 1, kv_last)
    soft_rest(1 - core)
    for h in range(heads):
        r = slice(h * tokens, (h + 1) * tokens)
        soft_ref[:, cut(h)] = (acc[r, :] / den[r, :]).astype(BF16)

    get_gate.wait()
    get_gain.wait()
    for h in range(heads):
        opened = jax.nn.sigmoid(gate[:, cut(h)].astype(F32))
        mixed[:, cut(h)] = mixed[:, cut(h)] * (gain_ref[:, cut(h)] * opened)
    each(nh - 1, lambda i: sum_copy(i).wait_recv())
    everyone = sums[...].reshape(nh * 8, tokens)
    eighth = jnp.full((nh * 8, HEAD_DIM), 0.125, F32)
    spread_sums = dot(everyone, eighth, TN, HIGH)
    inverse = lax.rsqrt(spread_sums / (heads * HEAD_DIM * nh) + NORM_EPS)
    for h in range(heads):
        lin_ref[:, cut(h)] = (mixed[:, cut(h)] * inverse).astype(BF16)

    each(n - 1, lambda i: log_copy(i).wait_send())

    def kv_sent(i):
        for part in range(2):
            kv_copy(i, part, sib).wait_send()

    each(chips, kv_sent)

    def fwd_sent(i):
        for part in range(2):
            fwd_copy(i, part, near(i) * 2 + core).wait_send()

    each(chips - 1, fwd_sent)
    mem_copy.wait_send()

    def tot_sent(i):
        @pl.when(i > chip)
        def _():
            tot_copy(i).wait_send()

    each(chips, tot_sent)
    ent_copy.wait_send()
    each(nh - 1, lambda i: sum_copy(i).wait_send())


def solution(mesh):
    n, nh = mesh.shape["seq"], mesh.shape["head"]
    chips = n // 2

    def step(lq, lk, lv, ld, gate, gain, sq, sk, sv, seg):
        tokens, width = lq.shape
        heads = width // HEAD_DIM
        half = heads // 2
        block = (tokens, width)
        square = (HEAD_DIM, HEAD_DIM)
        dma = pltpu.SemaphoreType.DMA
        anywhere = pl.BlockSpec(memory_space=pltpu.HBM)
        operands = [
            pltpu.with_memory_space_constraint(a, pltpu.HBM)
            for a in (lq, lk, lv, ld, gate, gain.reshape(1, width), sq, sk, sv, seg)
        ]
        results = pl.pallas_call(
            functools.partial(kernel, n, nh),
            out_shape=[jax.ShapeDtypeStruct(block, BF16)] * 2,
            in_specs=[anywhere] * 10,
            out_specs=[pl.BlockSpec(memory_space=pltpu.VMEM)] * 2,
            scratch_shapes=[
                pltpu.VMEM(block, BF16),
                pltpu.VMEM(block, BF16),
                pltpu.VMEM(block, BF16),
                pltpu.VMEM(block, BF16),
                pltpu.VMEM(block, BF16),
                pltpu.VMEM((heads * tokens, HEAD_DIM), BF16),
                pltpu.VMEM((n, 2, tokens, HEAD_DIM), BF16),
                pltpu.VMEM((n, heads, tokens), F32),
                pltpu.VMEM((heads,) + square, BF16),
                pltpu.VMEM((heads,) + square, BF16),
                pltpu.VMEM((half,) + square, BF16),
                pltpu.VMEM((chips, half) + square, BF16),
                pltpu.VMEM((half,) + square, F32),
                pltpu.VMEM((half,) + square, BF16),
                pltpu.VMEM((half,) + square, BF16),
                pltpu.VMEM(block, F32),
                pltpu.VMEM((nh, 8, tokens), F32),
                pltpu.VMEM((heads * tokens, HEAD_DIM), F32),
                pltpu.VMEM((heads * tokens, HEAD_DIM), F32),
                pltpu.VMEM((heads * tokens, HEAD_DIM), F32),
                pltpu.VMEM((1, width), F32),
                pltpu.SMEM((n,), jnp.int32),
                dma((10,)),
                dma((chips, 2)),
                dma((2 * chips, 2)),
                dma((chips, 2)),
                dma((n,)),
                dma((n,)),
                dma,
                dma,
                dma((chips,)),
                dma((chips,)),
                dma,
                dma,
                dma((nh,)),
                dma((nh,)),
            ],
            compiler_params=pltpu.CompilerParams(
                collective_id=0,
                has_side_effects=True,
                vmem_limit_bytes=40 * 1024 * 1024,
            ),
        )(*operands)
        return tuple(results)

    return jax.shard_map(
        step,
        mesh=mesh,
        in_specs=(
            P("seq", "head"),
            P("seq", "head"),
            P("seq", "head"),
            P("head", "seq"),
            P("seq", "head"),
            P("head"),
            P("seq", "head"),
            P("seq", None),
            P("seq", None),
            P(),
        ),
        out_specs=(P("seq", "head"), P("seq", "head")),
        check_vma=False,
    )
```

```python
import functools

import jax
import jax.numpy as jnp
from jax import lax
from jax.experimental import pallas as pl
from jax.experimental.pallas import tpu as pltpu
from jax.sharding import PartitionSpec as P

HEAD_DIM = 128
Q_PER_KV = 8
NORM_EPS = 1e-06
LOG2E = 1.4426950408889634
MESH = pl.DeviceIdType.MESH
F32 = jnp.float32
BF16 = jnp.bfloat16
NT = (((1,), (1,)), ((), ()))
TN = (((0,), (0,)), ((), ()))
HIGH = lax.Precision.HIGHEST


def dot(a, b, dims=(((1,), (0,)), ((), ())), precision=None):
    return lax.dot_general(a, b, dims, preferred_element_type=F32, precision=precision)


def each(count, body):
    if count <= 8:
        for i in range(count):
            body(i)
    else:
        lax.fori_loop(0, count, lambda i, _: (body(i), 0)[1], 0)


def kernel(
    n,
    nh,
    lq_hbm,
    lk_hbm,
    lv_hbm,
    ld_hbm,
    gate_hbm,
    gain_hbm,
    sq_hbm,
    sk_hbm,
    sv_hbm,
    seg_hbm,
    lin_ref,
    soft_ref,
    lq,
    lk,
    lv,
    gate,
    sq,
    qs,
    kv,
    logs,
    mem_own,
    mem_sib,
    tot_own,
    tot_all,
    pre,
    ent_own,
    ent_sib,
    mixed,
    sums,
    top,
    acc,
    den,
    gain_ref,
    seg_ref,
    in_sem,
    kv_send,
    kv_recv,
    fwd_send,
    log_send,
    log_recv,
    mem_send,
    mem_recv,
    tot_send,
    tot_recv,
    ent_send,
    ent_recv,
    sum_send,
    sum_recv,
):
    chips = n // 2
    me = lax.axis_index("seq")
    col = lax.axis_index("head")
    chip, core = me // 2, me % 2
    sib = chip * 2 + 1 - core
    tokens = lq.shape[0]
    heads = lq.shape[1] // HEAD_DIM
    half = heads // 2
    share = pl.multiple_of((col * heads // Q_PER_KV) * HEAD_DIM, HEAD_DIM)

    barrier = pltpu.get_barrier_semaphore()

    def greet(i):
        pl.semaphore_signal(
            barrier, inc=1, device_id=((me + 1 + i) % n, col), device_id_type=MESH
        )

    def greet_col(i):
        pl.semaphore_signal(
            barrier, inc=1, device_id=(me, (col + 1 + i) % nh), device_id_type=MESH
        )

    each(n - 1, greet)
    each(nh - 1, greet_col)

    def local(src, dst, at):
        copy = pltpu.make_async_copy(src, dst, in_sem.at[at])
        copy.start()
        return copy

    get_ld = local(ld_hbm, logs.at[me], 0)
    get_lk = local(lk_hbm, lk, 1)
    get_lv = local(lv_hbm, lv, 2)
    get_lq = local(lq_hbm, lq, 3)
    get_sk = local(sk_hbm.at[:, pl.ds(share, HEAD_DIM)], kv.at[me, 0], 4)
    get_sv = local(sv_hbm.at[:, pl.ds(share, HEAD_DIM)], kv.at[me, 1], 5)
    get_sq = local(sq_hbm, sq, 6)
    get_gate = local(gate_hbm, gate, 7)
    get_gain = local(gain_hbm, gain_ref, 8)
    get_seg = local(seg_hbm, seg_ref, 9)

    def remote(src, dst, send, recv, seq_to, col_to):
        return pltpu.make_async_remote_copy(
            src_ref=src,
            dst_ref=dst,
            send_sem=send,
            recv_sem=recv,
            device_id=(seq_to, col_to),
            device_id_type=MESH,
        )

    get_ld.wait()
    rows = lax.broadcasted_iota(jnp.int32, (tokens, tokens), 0)
    cols = lax.broadcasted_iota(jnp.int32, (tokens, tokens), 1)
    causal = rows >= cols
    lower = jnp.where(causal, 1.0, 0.0).astype(F32)
    decay = logs[me]
    cum_row = dot(decay, lower, NT, HIGH)
    cum_col = dot(lower, decay, NT, HIGH)
    tail = jnp.exp(cum_col[tokens - 1 : tokens, :] - cum_col)
    lift = jnp.exp(cum_col)

    get_sk.wait()
    get_sv.wait()
    pl.semaphore_wait(barrier, n - 1 + nh - 1)

    def log_copy(send, recv, to):
        return remote(
            logs.at[me], logs.at[me], log_send.at[send], log_recv.at[recv], to, col
        )

    def log_far(i, other):
        to = ((chip + 1 + i) % chips) * 2 + other
        return log_copy(2 * i + other, 2 * i + core, to)

    def log_came(i, other):
        return log_copy(2 * i, 2 * i + other, sib)

    log_near = log_copy(n - 1, n - 1, sib)

    def kv_copy(i, part, to):
        return remote(
            kv.at[me, part],
            kv.at[me, part],
            kv_send.at[i, part],
            kv_recv.at[i, part],
            to,
            col,
        )

    def far(i):
        return ((chip + 1 + i) % chips) * 2 + core

    def near(i):
        return (chip + chips - 1 - i) % chips

    log_near.start()

    def kv_go(i):
        kv_copy(i, 0, far(i)).start()
        kv_copy(i, 1, far(i)).start()

    each(chips - 1, kv_go)
    kv_copy(chips - 1, 0, sib).start()
    kv_copy(chips - 1, 1, sib).start()

    def cut(h):
        return slice(h * HEAD_DIM, (h + 1) * HEAD_DIM)

    get_lk.wait()
    get_lv.wait()
    for h in range(heads):
        weighted = (lk[:, cut(h)].astype(F32) * tail[:, h : h + 1]).astype(BF16)
        mem_own[h] = dot(weighted, lv[:, cut(h)], TN).astype(BF16)
    mem_copy = remote(mem_own, mem_sib, mem_send, mem_recv, sib, col)
    mem_copy.start()

    def log_go(i):
        log_far(i, 0).start()
        log_far(i, 1).start()

    each(chips - 1, log_go)

    get_lq.wait()
    for h in range(heads):
        scores = dot(lq[:, cut(h)], lk[:, cut(h)], NT)
        spread = cum_col[:, h : h + 1] - cum_row[h : h + 1, :]
        weight = jnp.where(causal, jnp.exp(jnp.where(causal, spread, 0.0)), 0.0)
        mixing = (scores * weight).astype(BF16)
        mixed[:, cut(h)] = dot(mixing, lv[:, cut(h)])

    log_near.wait_recv()

    def total(i):
        return jnp.sum(logs[i], axis=1, keepdims=True)

    odd_decay = jnp.exp(total(chip * 2 + 1))
    first = core.astype(F32)
    mem_copy.wait_recv()
    for p in range(half):
        h = core * half + p
        factor = jnp.where(core == 0, odd_decay[p : p + 1], odd_decay[half + p : half + p + 1])
        mine = mem_own[h].astype(F32)
        other = mem_sib[h].astype(F32)
        early = jnp.where(first > 0.5, other, mine)
        late = jnp.where(first > 0.5, mine, other)
        tot_own[p] = (factor * early + late).astype(BF16)

    def tot_copy(i):
        return remote(
            tot_own,
            tot_all.at[chip],
            tot_send.at[i],
            tot_recv.at[chip],
            i * 2 + core,
            col,
        )

    def tot_go(i):
        @pl.when(i > chip)
        def _():
            tot_copy(i).start()

    each(chips, tot_go)

    scale = HEAD_DIM ** (-0.5) * LOG2E
    get_seg.wait()
    own_segment = seg_ref[me]
    get_sq.wait()
    for h in range(heads):
        qs[h * tokens : (h + 1) * tokens, :] = sq[:, cut(h)]
    ones = jnp.ones((tokens, HEAD_DIM), BF16)

    def soft_group(owners, first=False):
        keys = jnp.concatenate([kv[o, 0] for o in owners], axis=0)
        values = jnp.concatenate(
            [jnp.concatenate([kv[o, 1], ones], axis=1) for o in owners], axis=0
        )
        raw = dot(qs[...], keys, NT)
        logits = []
        for j, owner in enumerate(owners):
            part = raw[:, j * tokens : (j + 1) * tokens] * scale
            if first and j == 0:
                shape = (heads, tokens, tokens)
                part = jnp.where(causal[None], part.reshape(shape), -1e30)
                part = part.reshape(heads * tokens, tokens)
            else:
                shown = seg_ref[owner] < own_segment
                part = part + jnp.where(shown, 0.0, -1e30).astype(F32)
            logits.append(part)
        peak = jnp.max(functools.reduce(jnp.maximum, logits), axis=1, keepdims=True)
        peak = jnp.broadcast_to(peak, (heads * tokens, HEAD_DIM))
        if not first:
            old = top[...]
            peak = jnp.maximum(old, peak)
            fade = jnp.exp2(old - peak)
        weights = [jnp.exp2(part - peak).astype(BF16) for part in logits]
        both = dot(jnp.concatenate(weights, axis=1), values)
        top[...] = peak
        if first:
            acc[...] = both[:, :HEAD_DIM]
            den[...] = both[:, HEAD_DIM:]
        else:
            acc[...] = acc[...] * fade + both[:, :HEAD_DIM]
            den[...] = den[...] * fade + both[:, HEAD_DIM:]

    def soft_rest(other):
        if chips <= 5:
            soft_group([near(i) * 2 + other for i in range(chips - 1)])
        else:
            each(chips - 1, lambda i: soft_group([near(i) * 2 + other]))

    kv_copy(chips - 1, 0, sib).wait_recv()
    kv_copy(chips - 1, 1, sib).wait_recv()
    soft_group([me, sib], True)

    def fwd_copy(i, part, owner):
        return remote(
            kv.at[owner, part],
            kv.at[owner, part],
            fwd_send.at[i, part],
            kv_recv.at[chips + i, part],
            sib,
            col,
        )

    def kv_pass(i):
        for part in range(2):
            kv_copy(i, part, far(i)).wait_recv()
            fwd_copy(i, part, near(i) * 2 + core).start()

    each(chips - 1, kv_pass)

    def log_get(i):
        log_came(i, 0).wait_recv()
        log_came(i, 1).wait_recv()

    each(chips - 1, log_get)
    pre[...] = jnp.zeros_like(pre)

    def join(i):
        @pl.when(i < chip)
        def _():
            remote(tot_own, tot_all.at[i], tot_send.at[i], tot_recv.at[i], sib, col).wait_recv()
            both = jnp.exp(total(i * 2) + total(i * 2 + 1))
            for p in range(half):
                factor = jnp.where(core == 0, both[p : p + 1], both[half + p : half + p + 1])
                pre[p] = factor * pre[p] + tot_all[i, p].astype(F32)

    each(chips, join)
    ent_own[...] = pre[...].astype(BF16)
    ent_copy = remote(ent_own, ent_sib, ent_send, ent_recv, sib, col)
    ent_copy.start()

    soft_rest(core)

    even_decay = jnp.exp(total(chip * 2))
    ent_copy.wait_recv()
    squares = jnp.zeros((tokens, HEAD_DIM), F32)
    for h in range(heads):
        pair, p = h // half, h % half
        here = jnp.where(core == pair, ent_own[p].astype(F32), ent_sib[p].astype(F32))
        later = even_decay[h : h + 1] * here + mem_sib[h].astype(F32)
        state = jnp.where(core == 0, here, later).astype(BF16)
        lifted = (lq[:, cut(h)].astype(F32) * lift[:, h : h + 1]).astype(BF16)
        value = mixed[:, cut(h)] + dot(lifted, state)
        mixed[:, cut(h)] = value
        squares = squares + value * value
    sums[col] = dot(jnp.ones((8, HEAD_DIM), F32), squares, NT, HIGH)

    def sum_copy(i):
        return remote(
            sums.at[col],
            sums.at[col],
            sum_send.at[i],
            sum_recv.at[i],
            me,
            (col + 1 + i) % nh,
        )

    each(nh - 1, lambda i: sum_copy(i).start())

    def kv_last(i):
        for part in range(2):
            fwd_copy(i, part, near(i) * 2 + core).wait_recv()

    each(chips - 1, kv_last)
    soft_rest(1 - core)
    for h in range(heads):
        r = slice(h * tokens, (h + 1) * tokens)
        soft_ref[:, cut(h)] = (acc[r, :] / den[r, :]).astype(BF16)

    get_gate.wait()
    get_gain.wait()
    for h in range(heads):
        opened = jax.nn.sigmoid(gate[:, cut(h)].astype(F32))
        mixed[:, cut(h)] = mixed[:, cut(h)] * (gain_ref[:, cut(h)] * opened)
    each(nh - 1, lambda i: sum_copy(i).wait_recv())
    everyone = sums[...].reshape(nh * 8, tokens)
    eighth = jnp.full((nh * 8, HEAD_DIM), 0.125, F32)
    spread_sums = dot(everyone, eighth, TN, HIGH)
    inverse = lax.rsqrt(spread_sums / (heads * HEAD_DIM * nh) + NORM_EPS)
    for h in range(heads):
        lin_ref[:, cut(h)] = (mixed[:, cut(h)] * inverse).astype(BF16)

    log_near.wait_send()

    def log_sent(i):
        log_far(i, 0).wait_send()
        log_far(i, 1).wait_send()

    each(chips - 1, log_sent)

    def kv_sent(i):
        for part in range(2):
            kv_copy(i, part, sib).wait_send()

    each(chips, kv_sent)

    def fwd_sent(i):
        for part in range(2):
            fwd_copy(i, part, near(i) * 2 + core).wait_send()

    each(chips - 1, fwd_sent)
    mem_copy.wait_send()

    def tot_sent(i):
        @pl.when(i > chip)
        def _():
            tot_copy(i).wait_send()

    each(chips, tot_sent)
    ent_copy.wait_send()
    each(nh - 1, lambda i: sum_copy(i).wait_send())


def solution(mesh):
    n, nh = mesh.shape["seq"], mesh.shape["head"]
    chips = n // 2

    def step(lq, lk, lv, ld, gate, gain, sq, sk, sv, seg):
        tokens, width = lq.shape
        heads = width // HEAD_DIM
        half = heads // 2
        block = (tokens, width)
        square = (HEAD_DIM, HEAD_DIM)
        dma = pltpu.SemaphoreType.DMA
        anywhere = pl.BlockSpec(memory_space=pltpu.HBM)
        operands = [
            pltpu.with_memory_space_constraint(a, pltpu.HBM)
            for a in (lq, lk, lv, ld, gate, gain.reshape(1, width), sq, sk, sv, seg)
        ]
        results = pl.pallas_call(
            functools.partial(kernel, n, nh),
            out_shape=[jax.ShapeDtypeStruct(block, BF16)] * 2,
            in_specs=[anywhere] * 10,
            out_specs=[pl.BlockSpec(memory_space=pltpu.VMEM)] * 2,
            scratch_shapes=[
                pltpu.VMEM(block, BF16),
                pltpu.VMEM(block, BF16),
                pltpu.VMEM(block, BF16),
                pltpu.VMEM(block, BF16),
                pltpu.VMEM(block, BF16),
                pltpu.VMEM((heads * tokens, HEAD_DIM), BF16),
                pltpu.VMEM((n, 2, tokens, HEAD_DIM), BF16),
                pltpu.VMEM((n, heads, tokens), F32),
                pltpu.VMEM((heads,) + square, BF16),
                pltpu.VMEM((heads,) + square, BF16),
                pltpu.VMEM((half,) + square, BF16),
                pltpu.VMEM((chips, half) + square, BF16),
                pltpu.VMEM((half,) + square, F32),
                pltpu.VMEM((half,) + square, BF16),
                pltpu.VMEM((half,) + square, BF16),
                pltpu.VMEM(block, F32),
                pltpu.VMEM((nh, 8, tokens), F32),
                pltpu.VMEM((heads * tokens, HEAD_DIM), F32),
                pltpu.VMEM((heads * tokens, HEAD_DIM), F32),
                pltpu.VMEM((heads * tokens, HEAD_DIM), F32),
                pltpu.VMEM((1, width), F32),
                pltpu.SMEM((n,), jnp.int32),
                dma((10,)),
                dma((chips, 2)),
                dma((2 * chips, 2)),
                dma((chips, 2)),
                dma((n,)),
                dma((n,)),
                dma,
                dma,
                dma((chips,)),
                dma((chips,)),
                dma,
                dma,
                dma((nh,)),
                dma((nh,)),
            ],
            compiler_params=pltpu.CompilerParams(
                collective_id=0,
                has_side_effects=True,
                vmem_limit_bytes=40 * 1024 * 1024,
            ),
        )(*operands)
        return tuple(results)

    return jax.shard_map(
        step,
        mesh=mesh,
        in_specs=(
            P("seq", "head"),
            P("seq", "head"),
            P("seq", "head"),
            P("head", "seq"),
            P("seq", "head"),
            P("head"),
            P("seq", "head"),
            P("seq", None),
            P("seq", None),
            P(),
        ),
        out_specs=(P("seq", "head"), P("seq", "head")),
        check_vma=False,
    )
```

```python
import functools

import jax
import jax.numpy as jnp
from jax import lax
from jax.experimental import pallas as pl
from jax.experimental.pallas import tpu as pltpu
from jax.sharding import PartitionSpec as P

HEAD_DIM = 128
Q_PER_KV = 8
NORM_EPS = 1e-06
LOG2E = 1.4426950408889634
MESH = pl.DeviceIdType.MESH
F32 = jnp.float32
BF16 = jnp.bfloat16
NT = (((1,), (1,)), ((), ()))
TN = (((0,), (0,)), ((), ()))
HIGH = lax.Precision.HIGHEST


def dot(a, b, dims=(((1,), (0,)), ((), ())), precision=None):
    return lax.dot_general(a, b, dims, preferred_element_type=F32, precision=precision)


def each(count, body):
    if count <= 8:
        for i in range(count):
            body(i)
    else:
        lax.fori_loop(0, count, lambda i, _: (body(i), 0)[1], 0)


def kernel(
    n,
    nh,
    lq_hbm,
    lk_hbm,
    lv_hbm,
    ld_hbm,
    gate_hbm,
    gain_hbm,
    sq_hbm,
    sk_hbm,
    sv_hbm,
    seg_hbm,
    lin_ref,
    soft_ref,
    lq,
    lk,
    lv,
    gate,
    sq,
    qs,
    kv,
    logs,
    mem_own,
    mem_sib,
    tot_own,
    tot_all,
    pre,
    ent_own,
    ent_sib,
    mixed,
    sums,
    top,
    acc,
    den,
    gain_ref,
    seg_ref,
    in_sem,
    kv_send,
    kv_recv,
    fwd_send,
    log_send,
    log_recv,
    mem_send,
    mem_recv,
    tot_send,
    tot_recv,
    ent_send,
    ent_recv,
    sum_send,
    sum_recv,
):
    chips = n // 2
    me = lax.axis_index("seq")
    col = lax.axis_index("head")
    chip, core = me // 2, me % 2
    sib = chip * 2 + 1 - core
    tokens = lq.shape[0]
    heads = lq.shape[1] // HEAD_DIM
    half = heads // 2
    share = pl.multiple_of((col * heads // Q_PER_KV) * HEAD_DIM, HEAD_DIM)

    barrier = pltpu.get_barrier_semaphore()

    def greet(i):
        pl.semaphore_signal(
            barrier, inc=1, device_id=((me + 1 + i) % n, col), device_id_type=MESH
        )

    def greet_col(i):
        pl.semaphore_signal(
            barrier, inc=1, device_id=(me, (col + 1 + i) % nh), device_id_type=MESH
        )

    each(n - 1, greet)
    each(nh - 1, greet_col)

    def local(src, dst, at):
        copy = pltpu.make_async_copy(src, dst, in_sem.at[at])
        copy.start()
        return copy

    get_ld = local(ld_hbm, logs.at[me], 0)
    get_lk = local(lk_hbm, lk, 1)
    get_lv = local(lv_hbm, lv, 2)
    get_lq = local(lq_hbm, lq, 3)
    get_sk = local(sk_hbm.at[:, pl.ds(share, HEAD_DIM)], kv.at[me, 0], 4)
    get_sv = local(sv_hbm.at[:, pl.ds(share, HEAD_DIM)], kv.at[me, 1], 5)
    get_sq = local(sq_hbm, sq, 6)
    get_gate = local(gate_hbm, gate, 7)
    get_gain = local(gain_hbm, gain_ref, 8)
    get_seg = local(seg_hbm, seg_ref, 9)

    def remote(src, dst, send, recv, seq_to, col_to):
        return pltpu.make_async_remote_copy(
            src_ref=src,
            dst_ref=dst,
            send_sem=send,
            recv_sem=recv,
            device_id=(seq_to, col_to),
            device_id_type=MESH,
        )

    get_ld.wait()
    rows = lax.broadcasted_iota(jnp.int32, (tokens, tokens), 0)
    cols = lax.broadcasted_iota(jnp.int32, (tokens, tokens), 1)
    causal = rows >= cols
    lower = jnp.where(causal, 1.0, 0.0).astype(F32)
    decay = logs[me]
    cum_row = dot(decay, lower, NT, HIGH)
    cum_col = dot(lower, decay, NT, HIGH)
    tail = jnp.exp(cum_col[tokens - 1 : tokens, :] - cum_col)
    lift = jnp.exp(cum_col)

    get_sk.wait()
    get_sv.wait()
    pl.semaphore_wait(barrier, n - 1 + nh - 1)

    def log_copy(send, recv, to):
        return remote(
            logs.at[me], logs.at[me], log_send.at[send], log_recv.at[recv], to, col
        )

    def log_far(i, other):
        to = ((chip + 1 + i) % chips) * 2 + other
        return log_copy(2 * i + other, 2 * i + core, to)

    def log_came(i, other):
        return log_copy(2 * i, 2 * i + other, sib)

    log_near = log_copy(n - 1, n - 1, sib)

    def kv_copy(i, part, to):
        return remote(
            kv.at[me, part],
            kv.at[me, part],
            kv_send.at[i, part],
            kv_recv.at[i, part],
            to,
            col,
        )

    def far(i):
        return ((chip + 1 + i) % chips) * 2 + core

    def near(i):
        return (chip + chips - 1 - i) % chips

    log_near.start()

    def kv_go(i):
        kv_copy(i, 0, far(i)).start()
        kv_copy(i, 1, far(i)).start()

    each(chips - 1, kv_go)
    kv_copy(chips - 1, 0, sib).start()
    kv_copy(chips - 1, 1, sib).start()

    def cut(h):
        return slice(h * HEAD_DIM, (h + 1) * HEAD_DIM)

    get_lk.wait()
    get_lv.wait()
    for h in range(heads):
        weighted = (lk[:, cut(h)].astype(F32) * tail[:, h : h + 1]).astype(BF16)
        mem_own[h] = dot(weighted, lv[:, cut(h)], TN).astype(BF16)
    mem_copy = remote(mem_own, mem_sib, mem_send, mem_recv, sib, col)
    mem_copy.start()

    def log_go(i):
        log_far(i, 0).start()
        log_far(i, 1).start()

    each(chips - 1, log_go)

    get_lq.wait()
    for h in range(heads):
        scores = dot(lq[:, cut(h)], lk[:, cut(h)], NT)
        spread = cum_col[:, h : h + 1] - cum_row[h : h + 1, :]
        weight = jnp.where(causal, jnp.exp(jnp.where(causal, spread, 0.0)), 0.0)
        mixing = (scores * weight).astype(BF16)
        mixed[:, cut(h)] = dot(mixing, lv[:, cut(h)])

    log_near.wait_recv()

    def total(i):
        return jnp.sum(logs[i], axis=1, keepdims=True)

    odd_decay = jnp.exp(total(chip * 2 + 1))
    first = core.astype(F32)
    mem_copy.wait_recv()
    for p in range(half):
        h = core * half + p
        factor = jnp.where(core == 0, odd_decay[p : p + 1], odd_decay[half + p : half + p + 1])
        mine = mem_own[h].astype(F32)
        other = mem_sib[h].astype(F32)
        early = jnp.where(first > 0.5, other, mine)
        late = jnp.where(first > 0.5, mine, other)
        tot_own[p] = (factor * early + late).astype(BF16)

    def tot_copy(i):
        return remote(
            tot_own,
            tot_all.at[chip],
            tot_send.at[i],
            tot_recv.at[chip],
            i * 2 + core,
            col,
        )

    def tot_go(i):
        @pl.when(i > chip)
        def _():
            tot_copy(i).start()

    each(chips, tot_go)

    scale = HEAD_DIM ** (-0.5) * LOG2E
    get_seg.wait()
    own_segment = seg_ref[me]
    get_sq.wait()
    for h in range(heads):
        qs[h * tokens : (h + 1) * tokens, :] = sq[:, cut(h)]
    ones = jnp.ones((tokens, HEAD_DIM), BF16)

    def soft_group(owners, first=False):
        keys = jnp.concatenate([kv[o, 0] for o in owners], axis=0)
        values = jnp.concatenate(
            [jnp.concatenate([kv[o, 1], ones], axis=1) for o in owners], axis=0
        )
        raw = dot(qs[...], keys, NT)
        logits = []
        for j, owner in enumerate(owners):
            part = raw[:, j * tokens : (j + 1) * tokens] * scale
            if first and j == 0:
                shape = (heads, tokens, tokens)
                part = jnp.where(causal[None], part.reshape(shape), -1e30)
                part = part.reshape(heads * tokens, tokens)
            else:
                shown = seg_ref[owner] < own_segment
                part = part + jnp.where(shown, 0.0, -1e30).astype(F32)
            logits.append(part)
        peak = jnp.max(functools.reduce(jnp.maximum, logits), axis=1, keepdims=True)
        peak = jnp.broadcast_to(peak, (heads * tokens, HEAD_DIM))
        if not first:
            old = top[...]
            peak = jnp.maximum(old, peak)
            fade = jnp.exp2(old - peak)
        weights = [jnp.exp2(part - peak).astype(BF16) for part in logits]
        both = dot(jnp.concatenate(weights, axis=1), values)
        top[...] = peak
        if first:
            acc[...] = both[:, :HEAD_DIM]
            den[...] = both[:, HEAD_DIM:]
        else:
            acc[...] = acc[...] * fade + both[:, :HEAD_DIM]
            den[...] = den[...] * fade + both[:, HEAD_DIM:]

    def soft_rest(other):
        if chips <= 5:
            soft_group([near(i) * 2 + other for i in range(chips - 1)])
        else:
            each(chips - 1, lambda i: soft_group([near(i) * 2 + other]))

    kv_copy(chips - 1, 0, sib).wait_recv()
    kv_copy(chips - 1, 1, sib).wait_recv()
    soft_group([me, sib], True)

    def fwd_copy(i, part, owner):
        return remote(
            kv.at[owner, part],
            kv.at[owner, part],
            fwd_send.at[i, part],
            kv_recv.at[chips + i, part],
            sib,
            col,
        )

    def kv_pass(i):
        for part in range(2):
            kv_copy(i, part, far(i)).wait_recv()
            fwd_copy(i, part, near(i) * 2 + core).start()


    def log_get(i):
        log_came(i, 0).wait_recv()
        log_came(i, 1).wait_recv()

    each(chips - 1, log_get)
    pre[...] = jnp.zeros_like(pre)

    def join(i):
        @pl.when(i < chip)
        def _():
            remote(tot_own, tot_all.at[i], tot_send.at[i], tot_recv.at[i], sib, col).wait_recv()
            both = jnp.exp(total(i * 2) + total(i * 2 + 1))
            for p in range(half):
                factor = jnp.where(core == 0, both[p : p + 1], both[half + p : half + p + 1])
                pre[p] = factor * pre[p] + tot_all[i, p].astype(F32)

    each(chips, join)
    ent_own[...] = pre[...].astype(BF16)
    ent_copy = remote(ent_own, ent_sib, ent_send, ent_recv, sib, col)
    ent_copy.start()
    each(chips - 1, kv_pass)

    soft_rest(core)

    even_decay = jnp.exp(total(chip * 2))
    ent_copy.wait_recv()
    squares = jnp.zeros((tokens, HEAD_DIM), F32)
    for h in range(heads):
        pair, p = h // half, h % half
        here = jnp.where(core == pair, ent_own[p].astype(F32), ent_sib[p].astype(F32))
        later = even_decay[h : h + 1] * here + mem_sib[h].astype(F32)
        state = jnp.where(core == 0, here, later).astype(BF16)
        lifted = (lq[:, cut(h)].astype(F32) * lift[:, h : h + 1]).astype(BF16)
        value = mixed[:, cut(h)] + dot(lifted, state)
        mixed[:, cut(h)] = value
        squares = squares + value * value
    sums[col] = dot(jnp.ones((8, HEAD_DIM), F32), squares, NT, HIGH)

    def sum_copy(i):
        return remote(
            sums.at[col],
            sums.at[col],
            sum_send.at[i],
            sum_recv.at[i],
            me,
            (col + 1 + i) % nh,
        )

    each(nh - 1, lambda i: sum_copy(i).start())

    def kv_last(i):
        for part in range(2):
            fwd_copy(i, part, near(i) * 2 + core).wait_recv()

    each(chips - 1, kv_last)
    soft_rest(1 - core)
    for h in range(heads):
        r = slice(h * tokens, (h + 1) * tokens)
        soft_ref[:, cut(h)] = (acc[r, :] / den[r, :]).astype(BF16)

    get_gate.wait()
    get_gain.wait()
    for h in range(heads):
        opened = jax.nn.sigmoid(gate[:, cut(h)].astype(F32))
        mixed[:, cut(h)] = mixed[:, cut(h)] * (gain_ref[:, cut(h)] * opened)
    each(nh - 1, lambda i: sum_copy(i).wait_recv())
    everyone = sums[...].reshape(nh * 8, tokens)
    eighth = jnp.full((nh * 8, HEAD_DIM), 0.125, F32)
    spread_sums = dot(everyone, eighth, TN, HIGH)
    inverse = lax.rsqrt(spread_sums / (heads * HEAD_DIM * nh) + NORM_EPS)
    for h in range(heads):
        lin_ref[:, cut(h)] = (mixed[:, cut(h)] * inverse).astype(BF16)

    log_near.wait_send()

    def log_sent(i):
        log_far(i, 0).wait_send()
        log_far(i, 1).wait_send()

    each(chips - 1, log_sent)

    def kv_sent(i):
        for part in range(2):
            kv_copy(i, part, sib).wait_send()

    each(chips, kv_sent)

    def fwd_sent(i):
        for part in range(2):
            fwd_copy(i, part, near(i) * 2 + core).wait_send()

    each(chips - 1, fwd_sent)
    mem_copy.wait_send()

    def tot_sent(i):
        @pl.when(i > chip)
        def _():
            tot_copy(i).wait_send()

    each(chips, tot_sent)
    ent_copy.wait_send()
    each(nh - 1, lambda i: sum_copy(i).wait_send())


def solution(mesh):
    n, nh = mesh.shape["seq"], mesh.shape["head"]
    chips = n // 2

    def step(lq, lk, lv, ld, gate, gain, sq, sk, sv, seg):
        tokens, width = lq.shape
        heads = width // HEAD_DIM
        half = heads // 2
        block = (tokens, width)
        square = (HEAD_DIM, HEAD_DIM)
        dma = pltpu.SemaphoreType.DMA
        anywhere = pl.BlockSpec(memory_space=pltpu.HBM)
        operands = [
            pltpu.with_memory_space_constraint(a, pltpu.HBM)
            for a in (lq, lk, lv, ld, gate, gain.reshape(1, width), sq, sk, sv, seg)
        ]
        results = pl.pallas_call(
            functools.partial(kernel, n, nh),
            out_shape=[jax.ShapeDtypeStruct(block, BF16)] * 2,
            in_specs=[anywhere] * 10,
            out_specs=[pl.BlockSpec(memory_space=pltpu.VMEM)] * 2,
            scratch_shapes=[
                pltpu.VMEM(block, BF16),
                pltpu.VMEM(block, BF16),
                pltpu.VMEM(block, BF16),
                pltpu.VMEM(block, BF16),
                pltpu.VMEM(block, BF16),
                pltpu.VMEM((heads * tokens, HEAD_DIM), BF16),
                pltpu.VMEM((n, 2, tokens, HEAD_DIM), BF16),
                pltpu.VMEM((n, heads, tokens), F32),
                pltpu.VMEM((heads,) + square, BF16),
                pltpu.VMEM((heads,) + square, BF16),
                pltpu.VMEM((half,) + square, BF16),
                pltpu.VMEM((chips, half) + square, BF16),
                pltpu.VMEM((half,) + square, F32),
                pltpu.VMEM((half,) + square, BF16),
                pltpu.VMEM((half,) + square, BF16),
                pltpu.VMEM(block, F32),
                pltpu.VMEM((nh, 8, tokens), F32),
                pltpu.VMEM((heads * tokens, HEAD_DIM), F32),
                pltpu.VMEM((heads * tokens, HEAD_DIM), F32),
                pltpu.VMEM((heads * tokens, HEAD_DIM), F32),
                pltpu.VMEM((1, width), F32),
                pltpu.SMEM((n,), jnp.int32),
                dma((10,)),
                dma((chips, 2)),
                dma((2 * chips, 2)),
                dma((chips, 2)),
                dma((n,)),
                dma((n,)),
                dma,
                dma,
                dma((chips,)),
                dma((chips,)),
                dma,
                dma,
                dma((nh,)),
                dma((nh,)),
            ],
            compiler_params=pltpu.CompilerParams(
                collective_id=0,
                has_side_effects=True,
                vmem_limit_bytes=40 * 1024 * 1024,
            ),
        )(*operands)
        return tuple(results)

    return jax.shard_map(
        step,
        mesh=mesh,
        in_specs=(
            P("seq", "head"),
            P("seq", "head"),
            P("seq", "head"),
            P("head", "seq"),
            P("seq", "head"),
            P("head"),
            P("seq", "head"),
            P("seq", None),
            P("seq", None),
            P(),
        ),
        out_specs=(P("seq", "head"), P("seq", "head")),
        check_vma=False,
    )
```
